32 devices in a mesh: tok: 4 (over z), tp: 4 (over y, x), grp: 2 (over core).
Axes of the slice: x: 2, y: 2, z: 4, core: 2. Of those that a mesh axis runs over, the one named last changes fastest.
Arguments:
- hidden: bfloat16 [1024, 6144], P(('tok', 'grp'), 'tp'), may hold values from -6 to 6
- gain: bfloat16 [6144], P('tp'), may hold values from 0.5 to 1.5
- expert_ids: int32 [1024, 2], P(('tok', 'grp')), may hold values from 0 to 3, all different within a row; in each aligned block of 128 rows (0 to 127, 128 to 255, ...) at most 80 rows name the same one
- gate_weights: float32 [1024, 2], P(('tok', 'grp')), may hold values from 0.1 to 0.9
- segment_ids: int32 [1024], P(('tok', 'grp')), may hold values from 0 to 7, never falling along the last dimension, each value on 1 to 384 neighbouring positions
- upstream: bfloat16 [1024, 6144], P(('tok', 'grp'), 'tp'), may hold values from -6 to 6
- w_gate: bfloat16 [4, 6144, 8192], P('tok', None, ('tp', 'grp')), may hold values from -0.078125 to 0.078125
- w_up: bfloat16 [4, 6144, 8192], P('tok', None, ('tp', 'grp')), may hold values from -0.078125 to 0.078125
- w_down: bfloat16 [4, 8192, 6144], P('tok', ('tp', 'grp')), may hold values from -0.0625 to 0.0625
Outputs:
- mixed: bfloat16 [1024, 6144], P(('tok', 'grp'), 'tp')
- importance: float32 [4, 8192], P('tok', ('tp', 'grp'))
The draws below stay inside these ranges and needn't reach their ends.
Inputs may be any that keep to these rules, and one draw needn't show every extreme that they name: `expert_ids`: each token names 2 different experts. Within the tokens of one token shard (aligned blocks of 128 rows) no expert is named by more than 80 tokens, and in some block one expert is named by exactly 80. `segment_ids`: never falling along the tokens; every document holds between 1 and 384 tokens.
All inputs are finite; a program needn't handle non-finite values.
Results may differ from the reference program's by a relative error of at most 0.0095.
Values may be sent and summed in bfloat16 or wider, within the bound.
A program may use at most 128 MiB of HBM per device.

```python
import math
import jax
import jax.numpy as jnp
import numpy as np
from jax import lax

D = 6144
TOP = 2
FW = 8192
RTOK = 128
EXPERTS = 4
CAP = 80
ROWS = 640
NDOCS = 8
TOKENS = 1024
N_TOK = 4
N_TP = 4
N_GRP = 2


def level_of(key, dims, pieces, least, high):
    factor_of = 1.0
    for dim, shards_of in pieces:
        draws = jax.random.uniform(jax.random.fold_in(jax.random.fold_in(key, 6), dim), (shards_of,), jnp.float32, least / len(pieces), high / len(pieces))
        factor_of = factor_of * jnp.repeat(jnp.exp(draws), dims[dim] // shards_of).reshape((-1,) + (1,) * (len(dims) - 1 - dim))
    return factor_of


def length_profile(amount, total, limit, lean):
    loads = [(1 << 20) // math.isqrt(standing ** lean) + 1 for standing in range(2, amount + 1)]
    spare, given = total - limit - (amount - 1), [1] * (amount - 1)
    while spare > 0:
        candidates = [i for i in range(amount - 1) if given[i] < limit]
        pool, budget = sum([loads[i] for i in candidates]), spare
        for i in candidates:
            extra = min(limit - given[i], max(1, budget * loads[i] // pool), spare)
            given[i] = given[i] + extra
            spare = spare - extra
    return np.array([limit] + given)


def uneven(own_key, number_of, total, bound, lean):
    if number_of == 2:
        one = jax.random.randint(own_key, (), max(1, total - bound), min(bound, total - 1) + 1)
        return jnp.stack([one, total - one])
    sizes = jnp.asarray(length_profile(number_of, total, bound, lean), jnp.int32)
    twos = (number_of - 1) // 2
    source_of, sink = sizes[1:1 + 2 * twos:2], sizes[2:2 + 2 * twos:2]
    room = jnp.minimum(source_of - 1, bound - sink)
    shifted = jax.random.randint(jax.random.fold_in(own_key, 1), (twos,), 0, 1 << 20) % (room + 1)
    sizes = sizes.at[1:1 + 2 * twos:2].set(source_of - shifted).at[2:2 + 2 * twos:2].set(sink + shifted)
    return sizes[jax.random.permutation(jax.random.fold_in(own_key, 2), number_of)]


def routed_block(own_key, own, number, rows, count, top, bound, skew):
    ranking = jax.random.permutation(own_key, count)
    packed, ordinary = portions_of(count, rows * top, bound, skew, True), portions_of(count, rows * top, bound, skew, False)
    places = jnp.arange(count)

    def named(lengths, turn):
        used = int((lengths > 0).sum())
        fixed = max(1, used // 4)
        shifted = fixed + (places - fixed + turn * (used - fixed)) % max(1, count - fixed)
        return jnp.zeros((count,), jnp.int32).at[ranking[jnp.where(places < fixed, places, shifted)]].set(jnp.asarray(lengths, jnp.int32))

    lengths = jnp.where(number % 4 == 0, named(packed, number // 4), named(ordinary, number - number // 4 - 1))
    mixed = jax.random.permutation(jax.random.fold_in(own, 3), count)
    donor, sink = mixed[0:count // 2 * 2:2], mixed[1:count // 2 * 2:2]
    margin = jnp.minimum(lengths[donor] - 1, bound - lengths[sink]) // 2
    margin = jnp.where((donor == ranking[0]) | (sink == ranking[0]) | (lengths[sink] == 0), 0, jnp.maximum(margin, 0))
    shifted = jax.random.randint(jax.random.fold_in(own, 4), (count // 2,), 0, 1 << 20) % (margin + 1)
    lengths = lengths.at[donor].add(-shifted).at[sink].add(shifted)
    items = jnp.searchsorted(jnp.cumsum(lengths), jnp.arange(rows * top), side="right").astype(jnp.int32)
    table = items.reshape(top, rows).T
    table = table[jax.random.permutation(jax.random.fold_in(own, 1), rows)]
    turn = jax.random.randint(jax.random.fold_in(own, 2), (rows, 1), 0, top)
    return jnp.take_along_axis(table, (jnp.arange(top)[None, :] + turn) % top, axis=1)


def portions_of(amount, total, bound, lean, full):
    loads = [(1 << 20) // math.isqrt(grade ** lean) + 1 for grade in range(1, amount + 1)]
    largest = bound if full else min(bound, max(-(-total // amount), total * loads[0] // sum(loads)))
    least = 1 if total - largest >= amount - 1 else 0
    given, rest = [largest] + [least] * (amount - 1), total - largest - least * (amount - 1)
    while rest > 0:
        candidates = [i for i in range(1, amount) if given[i] < largest] or [i for i in range(1, amount) if given[i] < bound]
        whole, left = sum([loads[i] for i in candidates]), rest
        for i in candidates:
            more = min(bound - given[i], max(1, left * loads[i] // whole), rest)
            given[i] = given[i] + more
            rest = rest - more
    return np.array(given)


def noise(rng, shape, width, most, shards=(), kind=jnp.bfloat16):
    drawn = jax.random.normal(rng, shape, jnp.float32) * width
    if len(shards) > 0:
        drawn = level_of(rng, shape, shards, -0.22, 0.18) * drawn
    return jnp.clip(drawn, min=-most, max=most).astype(kind)


def setup_inputs(seed: int = 0) -> dict:
    key_list = jax.random.split(jax.random.key(seed), 10)
    hidden = noise(key_list[0], (TOKENS, D), 1.0, 6.0, ((0, 8), (1, 4)))
    gain = jnp.clip(1.0 + 0.1 * jax.random.normal(key_list[1], (D,), jnp.float32), 0.5, 1.5).astype(jnp.bfloat16)
    expert_ids_keys = jax.random.split(jax.random.fold_in(key_list[2], 1), TOKENS // RTOK)
    expert_ids_turns = jax.random.permutation(jax.random.fold_in(key_list[2], 3), TOKENS // RTOK)
    expert_ids = jax.vmap(lambda own, number: routed_block(jax.random.fold_in(key_list[2], 2), own, number, RTOK, EXPERTS, TOP, CAP, 2))(expert_ids_keys, expert_ids_turns).reshape((TOKENS, TOP))
    gate_weights = jnp.clip(0.1 + 0.79999997 * jax.random.uniform(key_list[3], (TOKENS, TOP), jnp.float32) ** level_of(key_list[3], (TOKENS, TOP), ((0, 8),), -0.2, 0.2), 0.1, 0.9)
    segment_ids = jnp.searchsorted(jnp.cumsum(uneven(key_list[4], NDOCS, TOKENS, 3 * RTOK, 2)), jnp.arange(TOKENS), side="right").astype(jnp.int32)
    upstream = noise(key_list[5], (TOKENS, D), 1.0, 6.0, ((0, 8), (1, 4)))
    w_gate = noise(key_list[6], (EXPERTS, D, FW), D ** -0.5, 0.078125, ((0, 4), (2, 8)))
    w_up = noise(key_list[7], (EXPERTS, D, FW), D ** -0.5, 0.078125, ((0, 4), (2, 8)))
    w_down = noise(key_list[8], (EXPERTS, FW, D), FW ** -0.5, 0.0625, ((0, 4), (1, 8)))
    return {"hidden": hidden, "gain": gain, "expert_ids": expert_ids, "gate_weights": gate_weights, "segment_ids": segment_ids, "upstream": upstream, "w_gate": w_gate, "w_up": w_up, "w_down": w_down}


def expert_pass(operands):
    rows_in, cot_in, gate_mat, up_mat, down_mat = operands
    gate_pre = jnp.dot(rows_in, gate_mat, preferred_element_type=jnp.float32)
    up_proj = jnp.dot(rows_in, up_mat, preferred_element_type=jnp.float32)
    sigmoid_gate = jax.nn.sigmoid(gate_pre)
    activated = gate_pre * sigmoid_gate
    hidden_act = (activated * up_proj).astype(jnp.bfloat16)
    block_width = FW // (N_TP * N_GRP)

    def add_block(total, index):
        start = (index * block_width).astype(jnp.int32)
        act_block = lax.dynamic_slice_in_dim(hidden_act, start, block_width, 1)
        down_block = lax.dynamic_slice_in_dim(down_mat, start, block_width, 0)
        part = jnp.dot(act_block, down_block, preferred_element_type=jnp.float32).astype(jnp.bfloat16)
        return (total + part.astype(jnp.float32), None)
    start_total = jnp.zeros((rows_in.shape[0], down_mat.shape[1]), jnp.float32)
    out_total, unused = lax.scan(add_block, start_total, jnp.arange(N_TP * N_GRP, dtype=jnp.int32))
    expert_out = out_total.astype(jnp.bfloat16)
    grad_act = lax.dot_general(cot_in, down_mat, (((1,), (1,)), ((), ())), preferred_element_type=jnp.float32)
    grad_gate = (grad_act * up_proj * sigmoid_gate * (1.0 + gate_pre * (1.0 - sigmoid_gate))).astype(jnp.bfloat16)
    grad_up = (grad_act * activated).astype(jnp.bfloat16)
    grad_wgate = lax.dot_general(rows_in, grad_gate, (((0,), (0,)), ((), ())), preferred_element_type=jnp.float32)
    grad_wup = lax.dot_general(rows_in, grad_up, (((0,), (0,)), ((), ())), preferred_element_type=jnp.float32)
    grad_wdown = lax.dot_general(hidden_act, cot_in, (((0,), (0,)), ((), ())), preferred_element_type=jnp.float32)
    scores = lax.optimization_barrier(jnp.sum(jnp.abs(grad_wgate * gate_mat.astype(jnp.float32)), axis=0))
    scores = scores + lax.optimization_barrier(jnp.sum(jnp.abs(grad_wup * up_mat.astype(jnp.float32)), axis=0))
    scores = scores + lax.optimization_barrier(jnp.sum(jnp.abs(grad_wdown * down_mat.astype(jnp.float32)), axis=1))
    return (expert_out, scores)

def reference(hidden, gain, expert_ids, gate_weights, segment_ids, upstream, w_gate, w_up, w_down):
    wide_hidden = hidden.astype(jnp.float32)
    squares = lax.optimization_barrier(jnp.sum(wide_hidden * wide_hidden, axis=1, keepdims=True))
    normed = (wide_hidden * lax.rsqrt(squares / D + 1e-05) * gain.astype(jnp.float32)).astype(jnp.bfloat16)
    documents = jnp.arange(NDOCS, dtype=jnp.int32)
    doc_onehot = (segment_ids[:, None] == documents[None, :]).astype(jnp.float32)
    doc_len = lax.optimization_barrier(jnp.sum(doc_onehot, axis=0))
    tok_len = lax.optimization_barrier(jnp.sum(doc_onehot * doc_len[None, :], axis=1))
    tok_weight = RTOK / tok_len
    scaled = gate_weights * tok_weight[:, None]
    cot_rows = (scaled[:, :, None] * upstream.astype(jnp.float32)[:, None, :]).astype(jnp.bfloat16)
    shard_ids = expert_ids.reshape(TOKENS // RTOK, RTOK * TOP)
    onehot = (shard_ids[:, :, None] == jnp.arange(EXPERTS, dtype=jnp.int32)[None, None, :]).astype(jnp.int32)
    before = jnp.cumsum(onehot, axis=1).astype(jnp.int32) - onehot
    slot_ids = lax.optimization_barrier(jnp.sum(before * onehot, axis=2)).astype(jnp.int32).reshape(TOKENS, TOP)
    shard_index = (jnp.arange(TOKENS, dtype=jnp.int32) // RTOK).astype(jnp.int32)
    source_tok = shard_index // N_GRP
    source_grp = shard_index % N_GRP
    row_ids = (source_grp * (N_TOK * CAP) + source_tok * CAP)[:, None] + slot_ids
    row_ids = row_ids.astype(jnp.int32)
    rows_in = jnp.zeros((EXPERTS, ROWS, D), jnp.bfloat16)
    rows_in = rows_in.at[expert_ids, row_ids].set(jnp.broadcast_to(normed[:, None, :], (TOKENS, TOP, D)))
    cot_in = jnp.zeros((EXPERTS, ROWS, D), jnp.bfloat16)
    cot_in = cot_in.at[expert_ids, row_ids].set(cot_rows)
    expert_out, scores = lax.map(expert_pass, (rows_in, cot_in, w_gate, w_up, w_down))
    picked = expert_out[expert_ids, row_ids].astype(jnp.float32)
    mixed = (wide_hidden + lax.optimization_barrier(jnp.sum(gate_weights[:, :, None] * picked, axis=1))).astype(jnp.bfloat16)
    importance = scores / TOKENS
    return (mixed, importance)
```

```python
import functools
import math

import jax
import jax.numpy as jnp
from jax import lax
from jax.experimental import pallas as pl
from jax.experimental.pallas import tpu as pltpu
from jax.sharding import PartitionSpec as P

MESH = pl.DeviceIdType.MESH
F32 = jnp.float32
BF16 = jnp.bfloat16


def snake(i, n):
    side = math.isqrt(n)
    if side * side != n:
        return i
    r = i // side
    q = i % side
    return r * side + q + (r % 2) * (side - 1 - 2 * q)


def tile_of(n, most):
    return most if n % most == 0 else n


def expert_kernel(
    E, T, G, C, W, H, NC, KB,
    blk_rows, blk_cot, wg, wu, wd,
    back, imp_gu, imp_dn,
    X, accg, accu, ga, act, act_t, dgu, wdv, part, part_in, sum_in, wbuf, xt,
    a2a_s, a2a_r, ring_s, ring_r, pair_s, pair_r, part_s, part_r, sum_s, sum_r, back_s, back_r, wsem, wdsem,
):
    s = lax.axis_index("tok")
    tp = lax.axis_index("tp")
    g = lax.axis_index("grp")
    p = snake(tp, T)
    right = snake((p + 1) % T, T)
    left = snake((p + T - 1) % T, T)
    other = 1 - g
    E2 = E // 2
    R2 = E2 * C
    HR = G * R2
    CR = R2 // NC
    D = T * W
    NK = W // KB
    blks = (blk_rows, blk_cot)

    def tokdev(k):
        return {"tok": (s + k) % E}

    def ringdev(d):
        return {"tp": right if d == 0 else left}

    pairdev = {"grp": other}

    barrier = pltpu.get_barrier_semaphore()
    for k in range(1, E):
        pl.semaphore_signal(barrier, inc=1, device_id=tokdev(k), device_id_type=MESH)
    for d in range(2):
        pl.semaphore_signal(barrier, inc=1, device_id=ringdev(d), device_id_type=MESH)
    pl.semaphore_signal(barrier, inc=1, device_id=pairdev, device_id_type=MESH)

    def wd_copy():
        return pltpu.make_async_copy(wd.at[0], wdv, wdsem)

    def fwd_copies(i, slot):
        h = i // (2 * NK)
        d = (i // NK) % 2
        k = i % NK
        off = d * h + (1 - d) * (T - h)
        t = snake((p + off) % T, T)
        start = pl.multiple_of(t * W + k * KB, KB)
        return [
            pltpu.make_async_copy(w.at[0, pl.ds(start, KB), :], wbuf.at[slot, m], wsem.at[slot, m])
            for m, w in enumerate((wg, wu))
        ]

    def grad_copies(j, slot):
        start = pl.multiple_of(j * KB, KB)
        return [
            pltpu.make_async_copy(w.at[0, pl.ds(start, KB), :], wbuf.at[slot, m], wsem.at[slot, m])
            for m, w in enumerate((wg, wu))
        ]

    for c in fwd_copies(0, 0):
        c.start()
    wd_copy().start()

    def group_rows(half, grp, c, n):
        return pl.ds(pl.multiple_of(half * HR + grp * R2 + c * n, 16), n)

    def a2a_copy(a, k):
        return pltpu.make_async_remote_copy(
            src_ref=blks[a].at[(s + k) % E],
            dst_ref=X.at[a, tp, group_rows(k % 2, g, k // 2, C), :],
            send_sem=a2a_s.at[a, k], recv_sem=a2a_r.at[a, k],
            device_id=tokdev(k), device_id_type=MESH,
        )

    def own_copy(a):
        return pltpu.make_async_copy(
            blks[a].at[s], X.at[a, tp, group_rows(0, g, 0, C), :], a2a_r.at[a, 0]
        )

    def slice_at(h, d):
        return snake((p + (h if d else T - h)) % T, T)

    def ring_copy(a, h, d, c, received=False):
        view = X.at[a, slice_at(h + 1 if received else h, d), group_rows(d, g, c, CR), :]
        return pltpu.make_async_remote_copy(
            src_ref=view, dst_ref=view,
            send_sem=ring_s.at[a, h, d, c], recv_sem=ring_r.at[a, h, d, c],
            device_id=ringdev(d), device_id_type=MESH,
        )

    def pair_copy(a, h, d, c, received=False):
        view = X.at[a, slice_at(h, d), group_rows(d, other if received else g, c, CR), :]
        return pltpu.make_async_remote_copy(
            src_ref=view, dst_ref=view,
            send_sem=pair_s.at[a, h, d, c], recv_sem=pair_r.at[a, h, d, c],
            device_id=pairdev, device_id_type=MESH,
        )

    pl.semaphore_wait(barrier, E + 2)
    for a in range(2):
        own_copy(a).start()
        for k in range(1, E):
            a2a_copy(a, k).start()

    def arrive(a, h):
        for c in range(NC):
            for d in range(2):
                if h == 0:
                    per = E2 // NC
                    for q in range(c * per, (c + 1) * per):
                        k = 2 * q + d
                        if k == 0:
                            own_copy(a).wait()
                        else:
                            a2a_copy(a, k).wait_recv()
                else:
                    ring_copy(a, h - 1, d, c, True).wait_recv()
                if h < T - 1:
                    ring_copy(a, h, d, c).start()
                pair_copy(a, h, d, c).start()

    def pair_arrive(a, h):
        for c in range(NC):
            for d in range(2):
                pair_copy(a, h, d, c, True).wait_recv()

    def rows_of(d):
        return pl.ds(pl.multiple_of(d * HR, 16), HR)

    def lanes(start, n, unit=128):
        return pl.ds(pl.multiple_of(start, unit), n)

    HN = tile_of(H, 256)
    WN = tile_of(W, 256)

    def zero(ref):
        def body(i, _):
            ref[pl.ds(pl.multiple_of(i * 16, 16), 16), :] = jnp.zeros((16, ref.shape[1]), F32)
            return 0
        lax.fori_loop(0, ref.shape[0] // 16, body, 0)

    def forward(h):
        pair_arrive(0, h)

        def body(i, _):
            slot = i % 2

            @pl.when(i + 1 < T * 2 * NK)
            def _():
                for c in fwd_copies(i + 1, 1 - slot):
                    c.start()

            for c in fwd_copies(i, slot):
                c.wait()
            d = (i // NK) % 2
            k = i % NK
            off = d * h + (1 - d) * (T - h)
            t = snake((p + off) % T, T)
            x = X[0, t, rows_of(d), lanes(k * KB, KB)]
            for m, acc in enumerate((accg, accu)):
                for n in range(H // HN):
                    cols = slice(n * HN, (n + 1) * HN)
                    acc[rows_of(d), cols] += jnp.dot(
                        x, wbuf[slot, m, :, cols], preferred_element_type=F32
                    )
            return 0

        lax.fori_loop(h * 2 * NK, (h + 1) * 2 * NK, body, 0)

    def activate():
        def body(i, _):
            rows = pl.ds(pl.multiple_of(i * 16, 16), 16)
            gate = accg[rows, :]
            up = accu[rows, :]
            sig = jax.nn.sigmoid(gate)
            silu = gate * sig
            act[rows, :] = (silu * up).astype(BF16)
            accg[rows, :] = up * sig * (1.0 + gate * (1.0 - sig))
            accu[rows, :] = silu
            return 0

        lax.fori_loop(0, 2 * HR // 16, body, 0)
        for n in range(H // 128):
            act_t[n * 128:(n + 1) * 128, :] = act[:, n * 128:(n + 1) * 128].T

    def gradients():
        def body(i, _):
            rows = pl.ds(pl.multiple_of(i * 16, 16), 16)
            grad = ga[rows, :]
            dgu[rows, 0:H] = (grad * accg[rows, :]).astype(BF16)
            dgu[rows, H:2 * H] = (grad * accu[rows, :]).astype(BF16)
            return 0

        lax.fori_loop(0, 2 * HR // 16, body, 0)

    def part_copy(k, d):
        return pltpu.make_async_remote_copy(
            src_ref=part.at[k, d, pl.ds(pl.multiple_of(other * R2, 16), R2), :],
            dst_ref=part_in.at[k, d],
            send_sem=part_s.at[k, d], recv_sem=part_r.at[k, d],
            device_id=pairdev, device_id_type=MESH,
        )

    def own_part(k, d):
        return part.at[k, d, pl.ds(pl.multiple_of(g * R2, 16), R2), :]

    def down(k):
        for d in range(2):
            t = snake((p + (1 + k if d else T - 1 - k)) % T, T)

            def body(n, _, d=d, t=t):
                part[k, d, :, lanes(n * WN, WN)] = jnp.dot(
                    act[d * HR:(d + 1) * HR, :], wdv[:, lanes(t * W + n * WN, WN)],
                    preferred_element_type=F32,
                ).astype(BF16)
                return 0

            lax.fori_loop(0, W // WN, body, 0)
            part_copy(k, d).start()

    def grad_act(h):
        pair_arrive(1, h)

        def body(i, _):
            d = i // (H // HN)
            n = i % (H // HN)
            off = d * h + (1 - d) * (T - h)
            t = snake((p + off) % T, T)
            ga[rows_of(d), lanes(n * HN, HN)] += lax.dot_general(
                X[1, t, rows_of(d), :], wdv[pl.ds(pl.multiple_of(n * HN, 16), HN), lanes(t * W, W)],
                (((1,), (1,)), ((), ())), preferred_element_type=F32,
            )
            return 0

        lax.fori_loop(0, 2 * (H // HN), body, 0)

    FT = tile_of(H, 512)

    def score_down(t):
        def body(i, _):
            f = i // (W // WN)
            n = i % (W // WN)
            fr = pl.ds(pl.multiple_of(f * FT, 16), FT)
            grad = jnp.dot(
                act_t[fr, :], X[1, t, :, lanes(n * WN, WN)], preferred_element_type=F32
            )
            value = jnp.abs(grad * wdv[fr, lanes(t * W + n * WN, WN)].astype(F32))
            total = imp_dn[fr, :]
            for q in range(WN // 128):
                total += value[:, q * 128:(q + 1) * 128]
            imp_dn[fr, :] = total
            return 0

        lax.fori_loop(0, (H // FT) * (W // WN), body, 0)

    NU = D // KB

    def score_gate_up(first, last):
        def body(j, _):
            slot = j % 2

            @pl.when(j + 1 < NU)
            def _():
                for c in grad_copies(j + 1, 1 - slot):
                    c.start()

            for c in grad_copies(j, slot):
                c.wait()
            for q in range(KB // 128):
                xt[q * 128:(q + 1) * 128, :] = X[0, j // NK, :, lanes((j % NK) * KB + q * 128, 128)].T
            for m in range(2):
                for n in range(H // HN):
                    grad = jnp.dot(
                        xt[...], dgu[:, m * H + n * HN:m * H + (n + 1) * HN],
                        preferred_element_type=F32,
                    )
                    value = jnp.abs(grad * wbuf[slot, m, :, n * HN:(n + 1) * HN].astype(F32))
                    imp_gu[:, n * HN:(n + 1) * HN] += jnp.sum(value.reshape(KB // 8, 8, HN), axis=0)
            return 0

        lax.fori_loop(first, last, body, 0)

    def sum_copy(k, d):
        return pltpu.make_async_remote_copy(
            src_ref=own_part(k, d), dst_ref=sum_in.at[k, d],
            send_sem=sum_s.at[k, d], recv_sem=sum_r.at[k, d],
            device_id=ringdev(d), device_id_type=MESH,
        )

    def back_rows(k):
        return part.at[T - 1, k % 2, pl.ds(pl.multiple_of(g * R2 + (k // 2) * C, 16), C), :]

    def back_copy(k):
        return pltpu.make_async_remote_copy(
            src_ref=back_rows(k), dst_ref=back.at[s],
            send_sem=back_s.at[k], recv_sem=back_r.at[k],
            device_id={"tok": (s + E - k) % E}, device_id_type=MESH,
        )

    def back_own():
        return pltpu.make_async_copy(back_rows(0), back.at[s], back_r.at[0])

    def reduce_step(k):
        for d in range(2):
            part_copy(k, d).wait_recv()
            if k > 0:
                sum_copy(k - 1, d).wait_recv()

            def body(i, _, d=d):
                rows = pl.ds(pl.multiple_of(g * R2 + i * 16, 16), 16)
                here = pl.ds(pl.multiple_of(i * 16, 16), 16)
                total = part[k, d, rows, :].astype(F32) + part_in[k, d, here, :].astype(F32)
                if k > 0:
                    total += sum_in[k - 1, d, here, :].astype(F32)
                part[k, d, rows, :] = total.astype(BF16)
                return 0

            lax.fori_loop(0, R2 // 16, body, 0)
            if k < T - 1:
                sum_copy(k, d).start()
        if k == T - 1:
            back_own().start()
            for q in range(1, E):
                back_copy(q).start()

    for ref in (accg, accu, ga):
        zero(ref)
    imp_gu[...] = jnp.zeros(imp_gu.shape, F32)
    imp_dn[...] = jnp.zeros(imp_dn.shape, F32)

    arrive(0, 0)
    for h in range(1, T):
        arrive(0, h)
        forward(h - 1)
        if h == 1:
            arrive(1, 0)
    forward(T - 1)
    for c in grad_copies(0, 0):
        c.start()
    activate()
    wd_copy().wait()
    for h in range(1, T):
        down(h - 1)
        arrive(1, h)
        grad_act(h - 1)
        if h == 1:
            score_down(tp)
        if h - 1 == T // 2:
            score_down(slice_at(T // 2, 0))
        if h == T - 1:
            down(T - 1)
        if h > 1:
            reduce_step(h - 2)
    grad_act(T - 1)
    reduce_step(T - 2)
    if T - 1 == T // 2:
        score_down(slice_at(T // 2, 0))
    gradients()
    score_gate_up(0, NU // 2)
    reduce_step(T - 1)
    score_gate_up(NU // 2, NU)
    for h in range(1, T):
        if h != T // 2:
            score_down(slice_at(h, 0))

    back_own().wait()
    for k in range(1, E):
        back_copy(k).wait()
        for a in range(2):
            a2a_copy(a, k).wait_send()
    for k in range(T):
        for d in range(2):
            part_copy(k, d).wait_send()
            if k < T - 1:
                sum_copy(k, d).wait_send()
            for a in range(2):
                for c in range(NC):
                    pair_copy(a, k, d, c).wait_send()
                    if k < T - 1:
                        ring_copy(a, k, d, c).wait_send()


def expert_call(block_rows, block_cot, w_gate, w_up, w_down):
    E, C, W = block_rows.shape
    T = lax.axis_size("tp")
    G = lax.axis_size("grp")
    H = w_gate.shape[2]
    D = w_gate.shape[1]
    NC = E // 2 if T <= 4 else 1
    KB = tile_of(W, 512)
    rows = G * E * C
    R2 = E // 2 * C
    dma = pltpu.SemaphoreType.DMA
    hbm = pl.BlockSpec(memory_space=pl.ANY)
    vmem = pl.BlockSpec(memory_space=pltpu.VMEM)
    return pl.pallas_call(
        functools.partial(expert_kernel, E, T, G, C, W, H, NC, KB),
        out_shape=(
            jax.ShapeDtypeStruct((E, C, W), BF16),
            jax.ShapeDtypeStruct((8, H), F32),
            jax.ShapeDtypeStruct((H, 128), F32),
        ),
        in_specs=[hbm] * 5,
        out_specs=(hbm, vmem, vmem),
        scratch_shapes=[
            pltpu.VMEM((2, T, rows, W), BF16),
            pltpu.VMEM((rows, H), F32),
            pltpu.VMEM((rows, H), F32),
            pltpu.VMEM((rows, H), F32),
            pltpu.VMEM((rows, H), BF16),
            pltpu.VMEM((H, rows), BF16),
            pltpu.VMEM((rows, 2 * H), BF16),
            pltpu.VMEM((H, D), BF16),
            pltpu.VMEM((T, 2, G * R2, W), BF16),
            pltpu.VMEM((T, 2, R2, W), BF16),
            pltpu.VMEM((T - 1, 2, R2, W), BF16),
            pltpu.VMEM((2, 2, KB, H), BF16),
            pltpu.VMEM((KB, rows), BF16),
            dma((2, E)), dma((2, E)),
            dma((2, T, 2, NC)), dma((2, T, 2, NC)),
            dma((2, T, 2, NC)), dma((2, T, 2, NC)),
            dma((T, 2)), dma((T, 2)),
            dma((T, 2)), dma((T, 2)),
            dma((E,)), dma((E,)),
            dma((2, 2)), dma,
        ],
        compiler_params=pltpu.CompilerParams(
            collective_id=0, has_side_effects=True, vmem_limit_bytes=64 * 1024 * 1024 - 65536
        ),
        cost_estimate=pl.CostEstimate(
            flops=14 * rows * D * H, bytes_accessed=6 * D * H * 2, transcendentals=rows * H
        ),
        name="expert_layer",
    )(block_rows, block_cot, w_gate, w_up, w_down)


def on_device(hidden, gain, expert_ids, gate_weights, segment_ids, upstream, w_gate, w_up, w_down):
    rows_here = hidden.shape[0]
    top_count = expert_ids.shape[1]
    experts = lax.axis_size("tok")
    groups = lax.axis_size("grp")
    capacity = -(-(5 * rows_here // (2 * experts)) // 16) * 16
    width = w_gate.shape[1]
    documents = jnp.arange(experts * groups, dtype=jnp.int32)
    doc_onehot = (segment_ids[:, None] == documents[None, :]).astype(F32)
    doc_len = lax.psum(jnp.sum(doc_onehot, axis=0), ("tok", "grp"))
    tok_len = jnp.sum(doc_onehot * doc_len[None, :], axis=1)
    tok_weight = rows_here / tok_len
    onehot = (
        expert_ids.reshape(-1)[:, None] == jnp.arange(experts, dtype=jnp.int32)[None, :]
    ).astype(jnp.int32)
    before = jnp.cumsum(onehot, axis=0) - onehot
    slot_ids = jnp.sum(before * onehot, axis=1).reshape(rows_here, top_count)
    targets = expert_ids * capacity + slot_ids
    all_slots = jnp.arange(experts * capacity, dtype=jnp.int32)
    matches = all_slots[:, None, None] == targets[None, :, :]
    placing = jnp.any(matches, axis=2).astype(BF16)
    scaled = gate_weights * tok_weight[:, None]
    slot_scale = jnp.sum(jnp.where(matches, scaled[None, :, :], 0.0), axis=(1, 2))
    wide_hidden = hidden.astype(F32)
    squares = lax.psum(jnp.sum(wide_hidden * wide_hidden, axis=1), "tp")
    scaling = lax.rsqrt(squares / width + 1e-05)
    normed = (wide_hidden * scaling[:, None] * gain.astype(F32)[None, :]).astype(BF16)
    block_rows = jnp.dot(placing, normed, preferred_element_type=F32).astype(BF16)
    block_cot = jnp.dot(placing, upstream, preferred_element_type=F32) * slot_scale[:, None]
    block_rows = block_rows.reshape(experts, capacity, -1)
    block_cot = block_cot.astype(BF16).reshape(experts, capacity, -1)
    back, imp_gu, imp_dn = expert_call(block_rows, block_cot, w_gate, w_up, w_down)
    scores = jnp.sum(imp_gu, axis=0) + jnp.sum(imp_dn, axis=1)
    importance = scores / (rows_here * experts * groups)
    returned = back.reshape(experts * capacity, -1)
    combined = jnp.zeros(hidden.shape, F32)
    for k in range(top_count):
        pick = (targets[:, k][:, None] == all_slots[None, :]).astype(BF16)
        combined += gate_weights[:, k][:, None] * jnp.dot(pick, returned, preferred_element_type=F32)
    mixed = (wide_hidden + combined).astype(BF16)
    return (mixed, importance[None, :])


def solution(mesh):
    placed = (
        P(("tok", "grp"), "tp"),
        P("tp"),
        P(("tok", "grp"), None),
        P(("tok", "grp"), None),
        P(("tok", "grp")),
        P(("tok", "grp"), "tp"),
        P("tok", None, ("tp", "grp")),
        P("tok", None, ("tp", "grp")),
        P("tok", ("tp", "grp"), None),
    )
    return jax.shard_map(
        on_device,
        mesh=mesh,
        in_specs=placed,
        out_specs=(P(("tok", "grp"), "tp"), P("tok", ("tp", "grp"))),
        check_vma=False,
    )
```

```python
import functools
import math

import jax
import jax.numpy as jnp
from jax import lax
from jax.experimental import pallas as pl
from jax.experimental.pallas import tpu as pltpu
from jax.sharding import PartitionSpec as P

MESH = pl.DeviceIdType.MESH
F32 = jnp.float32
BF16 = jnp.bfloat16


def snake(i, n):
    side = math.isqrt(n)
    if side * side != n:
        return i
    r = i // side
    q = i % side
    return r * side + q + (r % 2) * (side - 1 - 2 * q)


def tile_of(n, most):
    return most if n % most == 0 else n


def expert_kernel(
    E, T, G, C, W, H, NC, KB,
    hidden, gain, upstream, placing, placed_gates, docs, picks, wg, wu, wd,
    mixed, imp,
    X, accg, accu, ga, act, act_t, dgu, wdv, part, part_in, sum_in, wbuf, xt,
    imp_gu, imp_dn, back, sq, doc,
    a2a_s, a2a_r, ring_s, ring_r, pair_s, pair_r, part_s, part_r, sum_s, sum_r, back_s, back_r, wsem, wdsem,
    sq_s, sq_r, doc_s, doc_r,
):
    s = lax.axis_index("tok")
    tp = lax.axis_index("tp")
    g = lax.axis_index("grp")
    p = snake(tp, T)
    right = snake((p + 1) % T, T)
    left = snake((p + T - 1) % T, T)
    other = 1 - g
    E2 = E // 2
    R2 = E2 * C
    HR = G * R2
    CR = R2 // NC
    D = T * W
    NK = W // KB
    N = hidden.shape[0]

    def tokdev(k):
        return {"tok": (s + k) % E}

    def ringdev(d):
        return {"tp": right if d == 0 else left}

    pairdev = {"grp": other}

    barrier = pltpu.get_barrier_semaphore()
    for k in range(1, E):
        pl.semaphore_signal(barrier, inc=1, device_id=tokdev(k), device_id_type=MESH)
        pl.semaphore_signal(
            barrier, inc=1, device_id={"tok": (s + k) % E, "grp": other}, device_id_type=MESH
        )
    for k in range(1, T):
        pl.semaphore_signal(barrier, inc=1, device_id={"tp": (tp + k) % T}, device_id_type=MESH)
    pl.semaphore_signal(barrier, inc=1, device_id=pairdev, device_id_type=MESH)

    def wd_copy():
        return pltpu.make_async_copy(wd.at[0], wdv, wdsem)

    def fwd_copies(i, slot):
        h = i // (2 * NK)
        d = (i // NK) % 2
        k = i % NK
        off = d * h + (1 - d) * (T - h)
        t = snake((p + off) % T, T)
        start = pl.multiple_of(t * W + k * KB, KB)
        return [
            pltpu.make_async_copy(w.at[0, pl.ds(start, KB), :], wbuf.at[slot, m], wsem.at[slot, m])
            for m, w in enumerate((wg, wu))
        ]

    def grad_copies(j, slot):
        start = pl.multiple_of(j * KB, KB)
        return [
            pltpu.make_async_copy(w.at[0, pl.ds(start, KB), :], wbuf.at[slot, m], wsem.at[slot, m])
            for m, w in enumerate((wg, wu))
        ]

    for c in fwd_copies(0, 0):
        c.start()
    wd_copy().start()

    def group_rows(half, grp, c, n):
        return pl.ds(pl.multiple_of(half * HR + grp * R2 + c * n, 16), n)

    def block(a, e):
        return part.at[T - 1, a, pl.ds(pl.multiple_of(e * C, 16), C), :]

    def a2a_copy(a, k):
        return pltpu.make_async_remote_copy(
            src_ref=block(a, (s + k) % E),
            dst_ref=X.at[a, tp, group_rows(k % 2, g, k // 2, C), :],
            send_sem=a2a_s.at[a, k], recv_sem=a2a_r.at[a, k],
            device_id=tokdev(k), device_id_type=MESH,
        )

    def own_copy(a):
        return pltpu.make_async_copy(
            block(a, s), X.at[a, tp, group_rows(0, g, 0, C), :], a2a_r.at[a, 0]
        )

    def slice_at(h, d):
        return snake((p + (h if d else T - h)) % T, T)

    def ring_copy(a, h, d, c, received=False):
        view = X.at[a, slice_at(h + 1 if received else h, d), group_rows(d, g, c, CR), :]
        return pltpu.make_async_remote_copy(
            src_ref=view, dst_ref=view,
            send_sem=ring_s.at[a, h, d, c], recv_sem=ring_r.at[a, h, d, c],
            device_id=ringdev(d), device_id_type=MESH,
        )

    def pair_copy(a, h, d, c, received=False):
        view = X.at[a, slice_at(h, d), group_rows(d, other if received else g, c, CR), :]
        return pltpu.make_async_remote_copy(
            src_ref=view, dst_ref=view,
            send_sem=pair_s.at[a, h, d, c], recv_sem=pair_r.at[a, h, d, c],
            device_id=pairdev, device_id_type=MESH,
        )

    def sq_copy(k):
        return pltpu.make_async_remote_copy(
            src_ref=sq.at[0], dst_ref=sq.at[k], send_sem=sq_s.at[k], recv_sem=sq_r.at[k],
            device_id={"tp": (tp + k) % T}, device_id_type=MESH,
        )

    def doc_copy(k):
        return pltpu.make_async_remote_copy(
            src_ref=doc.at[0], dst_ref=doc.at[k], send_sem=doc_s.at[k], recv_sem=doc_r.at[k],
            device_id={"tok": (s + k // G) % E, "grp": (g + k % G) % G}, device_id_type=MESH,
        )

    def send_blocks(a):
        own_copy(a).start()
        for k in range(1, E):
            a2a_copy(a, k).start()

    def lane_sum(value):
        return jnp.sum(value, axis=1, keepdims=True)

    def exchange_sums():
        total = jnp.zeros((N, 128), F32)
        for n in range(W // 128):
            value = hidden[:, n * 128:(n + 1) * 128].astype(F32)
            total += value * value
        sq[0] = jnp.broadcast_to(lane_sum(total), (N, 128))
        counts = jnp.sum(docs[...].astype(F32), axis=0, keepdims=True)
        doc[0] = jnp.broadcast_to(counts, (8, 128))
        pl.semaphore_wait(barrier, 2 * (E - 1) + T)
        for k in range(1, T):
            sq_copy(k).start()
        for k in range(1, E * G):
            doc_copy(k).start()

    def place_rows():
        total = sq[0]
        for k in range(1, T):
            sq_copy(k).wait_recv()
            total += sq[k]
        scaling = lax.rsqrt(total / D + 1e-05)
        where = placing[...]
        for n in range(W // 128):
            cols = slice(n * 128, (n + 1) * 128)
            normed = (hidden[:, cols].astype(F32) * scaling * gain[:, cols].astype(F32)).astype(BF16)
            part[T - 1, 0, :, cols] = jnp.dot(where, normed, preferred_element_type=F32).astype(BF16)

    def place_cot():
        lengths = doc[0]
        for k in range(1, E * G):
            doc_copy(k).wait_recv()
            lengths += doc[k]
        where = placing[...]
        slot_docs = jnp.dot(where, docs[...], preferred_element_type=F32)
        slot_len = lane_sum(slot_docs * lengths[0:1, :])
        weight = jnp.where(slot_len > 0.0, N / jnp.maximum(slot_len, 1.0), 0.0)
        scale = lane_sum(placed_gates[...]) * weight
        CW = tile_of(W, 256)
        for n in range(W // CW):
            cols = slice(n * CW, (n + 1) * CW)
            value = jnp.dot(where, upstream[:, cols], preferred_element_type=F32)
            part[T - 1, 1, :, cols] = (value * scale).astype(BF16)

    def combine():
        back_own().wait()
        for k in range(1, E):
            back_copy(k).wait_recv()
        CW = tile_of(W, 256)
        ways = []
        for k in range(picks.shape[0]):
            pick = picks[k]
            ways.append((jnp.where(pick != 0.0, 1.0, 0.0).astype(BF16), lane_sum(pick)))
        for n in range(W // CW):
            cols = slice(n * CW, (n + 1) * CW)
            total = jnp.zeros((N, CW), F32)
            for where, gate in ways:
                total += gate * jnp.dot(where, back[:, cols], preferred_element_type=F32)
            mixed[:, cols] = (hidden[:, cols].astype(F32) + total).astype(BF16)

    def arrive(a, h):
        for c in range(NC):
            for d in range(2):
                if h == 0:
                    per = E2 // NC
                    for q in range(c * per, (c + 1) * per):
                        k = 2 * q + d
                        if k == 0:
                            own_copy(a).wait()
                        else:
                            a2a_copy(a, k).wait_recv()
                else:
                    ring_copy(a, h - 1, d, c, True).wait_recv()
                if h < T - 1:
                    ring_copy(a, h, d, c).start()
                pair_copy(a, h, d, c).start()

    def pair_arrive(a, h):
        for c in range(NC):
            for d in range(2):
                pair_copy(a, h, d, c, True).wait_recv()

    def rows_of(d):
        return pl.ds(pl.multiple_of(d * HR, 16), HR)

    def lanes(start, n, unit=128):
        return pl.ds(pl.multiple_of(start, unit), n)

    HN = tile_of(H, 256)
    WN = tile_of(W, 256)

    def zero(ref):
        def body(i, _):
            ref[pl.ds(pl.multiple_of(i * 16, 16), 16), :] = jnp.zeros((16, ref.shape[1]), F32)
            return 0
        lax.fori_loop(0, ref.shape[0] // 16, body, 0)

    def forward(h):
        pair_arrive(0, h)

        def body(i, _):
            slot = i % 2

            @pl.when(i + 1 < T * 2 * NK)
            def _():
                for c in fwd_copies(i + 1, 1 - slot):
                    c.start()

            for c in fwd_copies(i, slot):
                c.wait()
            d = (i // NK) % 2
            k = i % NK
            off = d * h + (1 - d) * (T - h)
            t = snake((p + off) % T, T)
            x = X[0, t, rows_of(d), lanes(k * KB, KB)]
            for m, acc in enumerate((accg, accu)):
                for n in range(H // HN):
                    cols = slice(n * HN, (n + 1) * HN)
                    acc[rows_of(d), cols] += jnp.dot(
                        x, wbuf[slot, m, :, cols], preferred_element_type=F32
                    )
            return 0

        lax.fori_loop(h * 2 * NK, (h + 1) * 2 * NK, body, 0)

    def activate():
        def body(i, _):
            rows = pl.ds(pl.multiple_of(i * 16, 16), 16)
            gate = accg[rows, :]
            up = accu[rows, :]
            sig = jax.nn.sigmoid(gate)
            silu = gate * sig
            act[rows, :] = (silu * up).astype(BF16)
            accg[rows, :] = up * sig * (1.0 + gate * (1.0 - sig))
            accu[rows, :] = silu
            return 0

        lax.fori_loop(0, 2 * HR // 16, body, 0)
        for n in range(H // 128):
            act_t[n * 128:(n + 1) * 128, :] = act[:, n * 128:(n + 1) * 128].T

    def gradients():
        def body(i, _):
            rows = pl.ds(pl.multiple_of(i * 16, 16), 16)
            grad = ga[rows, :]
            dgu[rows, 0:H] = (grad * accg[rows, :]).astype(BF16)
            dgu[rows, H:2 * H] = (grad * accu[rows, :]).astype(BF16)
            return 0

        lax.fori_loop(0, 2 * HR // 16, body, 0)

    def part_copy(k, d):
        return pltpu.make_async_remote_copy(
            src_ref=part.at[k, d, pl.ds(pl.multiple_of(other * R2, 16), R2), :],
            dst_ref=part_in.at[k, d],
            send_sem=part_s.at[k, d], recv_sem=part_r.at[k, d],
            device_id=pairdev, device_id_type=MESH,
        )

    def own_part(k, d):
        return part.at[k, d, pl.ds(pl.multiple_of(g * R2, 16), R2), :]

    def down(k):
        for d in range(2):
            t = snake((p + (1 + k if d else T - 1 - k)) % T, T)

            def body(n, _, d=d, t=t):
                part[k, d, :, lanes(n * WN, WN)] = jnp.dot(
                    act[d * HR:(d + 1) * HR, :], wdv[:, lanes(t * W + n * WN, WN)],
                    preferred_element_type=F32,
                ).astype(BF16)
                return 0

            lax.fori_loop(0, W // WN, body, 0)
            part_copy(k, d).start()

    def grad_act(h):
        pair_arrive(1, h)

        def body(i, _):
            d = i // (H // HN)
            n = i % (H // HN)
            off = d * h + (1 - d) * (T - h)
            t = snake((p + off) % T, T)
            ga[rows_of(d), lanes(n * HN, HN)] += lax.dot_general(
                X[1, t, rows_of(d), :], wdv[pl.ds(pl.multiple_of(n * HN, 16), HN), lanes(t * W, W)],
                (((1,), (1,)), ((), ())), preferred_element_type=F32,
            )
            return 0

        lax.fori_loop(0, 2 * (H // HN), body, 0)

    FT = tile_of(H, 512)

    def score_down(t):
        def body(i, _):
            f = i // (W // WN)
            n = i % (W // WN)
            fr = pl.ds(pl.multiple_of(f * FT, 16), FT)
            grad = jnp.dot(
                act_t[fr, :], X[1, t, :, lanes(n * WN, WN)], preferred_element_type=F32
            )
            value = jnp.abs(grad * wdv[fr, lanes(t * W + n * WN, WN)].astype(F32))
            total = imp_dn[fr, :]
            for q in range(WN // 128):
                total += value[:, q * 128:(q + 1) * 128]
            imp_dn[fr, :] = total
            return 0

        lax.fori_loop(0, (H // FT) * (W // WN), body, 0)

    NU = D // KB

    def score_gate_up(first, last):
        def body(j, _):
            slot = j % 2

            @pl.when(j + 1 < NU)
            def _():
                for c in grad_copies(j + 1, 1 - slot):
                    c.start()

            for c in grad_copies(j, slot):
                c.wait()
            for q in range(KB // 128):
                xt[q * 128:(q + 1) * 128, :] = X[0, j // NK, :, lanes((j % NK) * KB + q * 128, 128)].T
            for m in range(2):
                for n in range(H // HN):
                    grad = jnp.dot(
                        xt[...], dgu[:, m * H + n * HN:m * H + (n + 1) * HN],
                        preferred_element_type=F32,
                    )
                    value = jnp.abs(grad * wbuf[slot, m, :, n * HN:(n + 1) * HN].astype(F32))
                    imp_gu[:, n * HN:(n + 1) * HN] += jnp.sum(value.reshape(KB // 8, 8, HN), axis=0)
            return 0

        lax.fori_loop(first, last, body, 0)

    def sum_copy(k, d):
        return pltpu.make_async_remote_copy(
            src_ref=own_part(k, d), dst_ref=sum_in.at[k, d],
            send_sem=sum_s.at[k, d], recv_sem=sum_r.at[k, d],
            device_id=ringdev(d), device_id_type=MESH,
        )

    def back_rows(k):
        return part.at[T - 1, k % 2, pl.ds(pl.multiple_of(g * R2 + (k // 2) * C, 16), C), :]

    def back_copy(k):
        return pltpu.make_async_remote_copy(
            src_ref=back_rows(k), dst_ref=back.at[pl.ds(pl.multiple_of(s * C, 16), C), :],
            send_sem=back_s.at[k], recv_sem=back_r.at[k],
            device_id={"tok": (s + E - k) % E}, device_id_type=MESH,
        )

    def back_own():
        return pltpu.make_async_copy(
            back_rows(0), back.at[pl.ds(pl.multiple_of(s * C, 16), C), :], back_r.at[0]
        )

    def reduce_step(k):
        for d in range(2):
            part_copy(k, d).wait_recv()
            if k > 0:
                sum_copy(k - 1, d).wait_recv()

            def body(i, _, d=d):
                rows = pl.ds(pl.multiple_of(g * R2 + i * 16, 16), 16)
                here = pl.ds(pl.multiple_of(i * 16, 16), 16)
                total = part[k, d, rows, :].astype(F32) + part_in[k, d, here, :].astype(F32)
                if k > 0:
                    total += sum_in[k - 1, d, here, :].astype(F32)
                part[k, d, rows, :] = total.astype(BF16)
                return 0

            lax.fori_loop(0, R2 // 16, body, 0)
            if k < T - 1:
                sum_copy(k, d).start()
        if k == T - 1:
            back_own().start()
            for q in range(1, E):
                back_copy(q).start()

    exchange_sums()
    for ref in (accg, accu, ga):
        zero(ref)
    imp_gu[...] = jnp.zeros(imp_gu.shape, F32)
    imp_dn[...] = jnp.zeros(imp_dn.shape, F32)
    place_rows()
    send_blocks(0)
    place_cot()

    arrive(0, 0)
    send_blocks(1)
    for h in range(1, T):
        arrive(0, h)
        forward(h - 1)
        if h == min(2, T - 1):
            arrive(1, 0)
    forward(T - 1)
    for c in grad_copies(0, 0):
        c.start()
    activate()
    wd_copy().wait()
    for a in range(2):
        for k in range(1, E):
            a2a_copy(a, k).wait_send()
    for h in range(1, T):
        down(h - 1)
        if h > 1:
            reduce_step(h - 2)
        arrive(1, h)
        grad_act(h - 1)
        if h == 1:
            score_down(tp)
    down(T - 1)
    grad_act(T - 1)
    gradients()
    first, second = NU // 4, NU // 4 + NU // 3
    score_gate_up(0, first)
    reduce_step(T - 2)
    score_gate_up(first, second)
    reduce_step(T - 1)
    score_gate_up(second, NU)
    for h in range(1, T):
        score_down(slice_at(h, 0))
    for n in range(H // 128):
        cols = slice(n * 128, (n + 1) * 128)
        value = jnp.sum(imp_gu[:, cols], axis=0, keepdims=True)
        value += jnp.sum(imp_dn[cols, :].T, axis=0, keepdims=True)
        imp[:, cols] = value / (N * E * G)
    combine()

    for k in range(1, E):
        back_copy(k).wait_send()
    for k in range(1, T):
        sq_copy(k).wait_send()
    for k in range(1, E * G):
        doc_copy(k).wait_send()
    for k in range(T):
        for d in range(2):
            part_copy(k, d).wait_send()
            if k < T - 1:
                sum_copy(k, d).wait_send()
            for a in range(2):
                for c in range(NC):
                    pair_copy(a, k, d, c).wait_send()
                    if k < T - 1:
                        ring_copy(a, k, d, c).wait_send()


def expert_call(hidden, gain, upstream, placing, placed_gates, docs, picks, w_gate, w_up, w_down):
    N, W = hidden.shape
    E = lax.axis_size("tok")
    C = placing.shape[0] // E
    T = lax.axis_size("tp")
    G = lax.axis_size("grp")
    H = w_gate.shape[2]
    D = w_gate.shape[1]
    NC = E // 2 if T <= 4 else 1
    KB = tile_of(W, 512)
    rows = G * E * C
    R2 = E // 2 * C
    dma = pltpu.SemaphoreType.DMA
    hbm = pl.BlockSpec(memory_space=pl.ANY)
    vmem = pl.BlockSpec(memory_space=pltpu.VMEM)
    return pl.pallas_call(
        functools.partial(expert_kernel, E, T, G, C, W, H, NC, KB),
        out_shape=(
            jax.ShapeDtypeStruct((N, W), BF16),
            jax.ShapeDtypeStruct((1, H), F32),
        ),
        in_specs=[vmem] * 7 + [hbm] * 3,
        out_specs=(vmem, vmem),
        scratch_shapes=[
            pltpu.VMEM((2, T, rows, W), BF16),
            pltpu.VMEM((rows, H), F32),
            pltpu.VMEM((rows, H), F32),
            pltpu.VMEM((rows, H), F32),
            pltpu.VMEM((rows, H), BF16),
            pltpu.VMEM((H, rows), BF16),
            pltpu.VMEM((rows, 2 * H), BF16),
            pltpu.VMEM((H, D), BF16),
            pltpu.VMEM((T, 2, G * R2, W), BF16),
            pltpu.VMEM((T, 2, R2, W), BF16),
            pltpu.VMEM((T - 1, 2, R2, W), BF16),
            pltpu.VMEM((2, 2, KB, H), BF16),
            pltpu.VMEM((KB, rows), BF16),
            pltpu.VMEM((8, H), F32),
            pltpu.VMEM((H, 128), F32),
            pltpu.VMEM((E * C, W), BF16),
            pltpu.VMEM((T, N, 128), F32),
            pltpu.VMEM((E * G, 8, 128), F32),
            dma((2, E)), dma((2, E)),
            dma((2, T, 2, NC)), dma((2, T, 2, NC)),
            dma((2, T, 2, NC)), dma((2, T, 2, NC)),
            dma((T, 2)), dma((T, 2)),
            dma((T, 2)), dma((T, 2)),
            dma((E,)), dma((E,)),
            dma((2, 2)), dma,
            dma((T,)), dma((T,)), dma((E * G,)), dma((E * G,)),
        ],
        compiler_params=pltpu.CompilerParams(
            collective_id=0, has_side_effects=True, vmem_limit_bytes=64 * 1024 * 1024 - 65536
        ),
        cost_estimate=pl.CostEstimate(
            flops=14 * rows * D * H, bytes_accessed=6 * D * H * 2, transcendentals=rows * H
        ),
        name="expert_layer",
    )(hidden, gain, upstream, placing, placed_gates, docs, picks, w_gate, w_up, w_down)


def on_device(hidden, gain, expert_ids, gate_weights, segment_ids, upstream, w_gate, w_up, w_down):
    rows_here = hidden.shape[0]
    top_count = expert_ids.shape[1]
    experts = lax.axis_size("tok")
    groups = lax.axis_size("grp")
    capacity = -(-(5 * rows_here // (2 * experts)) // 16) * 16
    width = w_gate.shape[1]
    places = jnp.arange(rows_here, dtype=jnp.int32)
    earlier = places[None, :] < places[:, None]
    all_slots = jnp.arange(experts * capacity, dtype=jnp.int32)
    docs = (segment_ids[:, None] == jnp.arange(128, dtype=jnp.int32)[None, :]).astype(BF16)
    placed_gates = jnp.zeros((experts * capacity, rows_here), F32)
    placing = jnp.zeros((experts * capacity, rows_here), jnp.bool_)
    picks = []
    for k in range(top_count):
        same = jnp.zeros((rows_here, rows_here), jnp.bool_)
        for other in range(top_count):
            same |= expert_ids[:, k][:, None] == expert_ids[:, other][None, :]
        slot = jnp.sum((same & earlier).astype(jnp.int32), axis=1)
        target = expert_ids[:, k] * capacity + slot
        match = all_slots[:, None] == target[None, :]
        placing |= match
        placed_gates += jnp.where(match, gate_weights[:, k][None, :], 0.0)
        picks.append(jnp.where(target[:, None] == all_slots[None, :], gate_weights[:, k][:, None], 0.0))
    return expert_call(
        hidden, gain[None, :], upstream, placing.astype(BF16), placed_gates, docs, jnp.stack(picks),
        w_gate, w_up, w_down,
    )


def solution(mesh):
    placed = (
        P(("tok", "grp"), "tp"),
        P("tp"),
        P(("tok", "grp"), None),
        P(("tok", "grp"), None),
        P(("tok", "grp")),
        P(("tok", "grp"), "tp"),
        P("tok", None, ("tp", "grp")),
        P("tok", None, ("tp", "grp")),
        P("tok", ("tp", "grp"), None),
    )
    return jax.shard_map(
        on_device,
        mesh=mesh,
        in_specs=placed,
        out_specs=(P(("tok", "grp"), "tp"), P("tok", ("tp", "grp"))),
        check_vma=False,
    )
```

```python
import functools
import math

import jax
import jax.numpy as jnp
from jax import lax
from jax.experimental import pallas as pl
from jax.experimental.pallas import tpu as pltpu
from jax.sharding import PartitionSpec as P

MESH = pl.DeviceIdType.MESH
F32 = jnp.float32
BF16 = jnp.bfloat16


def snake(i, n):
    side = math.isqrt(n)
    if side * side != n:
        return i
    r = i // side
    q = i % side
    return r * side + q + (r % 2) * (side - 1 - 2 * q)


def tile_of(n, most):
    return most if n % most == 0 else n


def expert_kernel(
    E, T, G, C, W, H, NC, KB,
    hidden, gain, upstream, placing, placed_gates, docs, picks, wg, wu, wd,
    mixed, imp,
    X, accg, accu, ga, act, act_t, dgu, wdv, part, part_in, sum_in, wbuf, xt,
    imp_gu, imp_dn, back, sq, doc,
    a2a_s, a2a_r, ring_s, ring_r, pair_s, pair_r, part_s, part_r, sum_s, sum_r, back_s, back_r, wsem, gsem, wdsem,
    sq_s, sq_r, doc_s, doc_r,
):
    s = lax.axis_index("tok")
    tp = lax.axis_index("tp")
    g = lax.axis_index("grp")
    p = snake(tp, T)
    right = snake((p + 1) % T, T)
    left = snake((p + T - 1) % T, T)
    other = 1 - g
    R = E * C
    CR = R // NC
    D = T * W
    NK = W // KB
    N = hidden.shape[0]
    W0 = -(-W // 256) * 128
    LOW = (0, W0)
    WIDE = (W0, W - W0)

    def part_lanes(d):
        return slice(LOW[d], LOW[d] + WIDE[d])

    def tokdev(k):
        return {"tok": (s + k) % E}

    def ringdev(d):
        return {"tp": right if d == 0 else left}

    pairdev = {"grp": other}

    barrier = pltpu.get_barrier_semaphore()
    for k in range(1, E):
        pl.semaphore_signal(barrier, inc=1, device_id=tokdev(k), device_id_type=MESH)
        pl.semaphore_signal(
            barrier, inc=1, device_id={"tok": (s + k) % E, "grp": other}, device_id_type=MESH
        )
    for k in range(1, T):
        pl.semaphore_signal(barrier, inc=1, device_id={"tp": (tp + k) % T}, device_id_type=MESH)
    pl.semaphore_signal(barrier, inc=1, device_id=pairdev, device_id_type=MESH)

    def slice_at(h, d):
        return snake((p + (h if d else T - h)) % T, T)

    def wd_copy():
        return pltpu.make_async_copy(wd.at[0], wdv, wdsem)

    def fwd_copy(u):
        h, d, m = u // 4, u // 2 % 2, u % 2
        start = pl.multiple_of(slice_at(h, d) * W + LOW[d], 128)
        return pltpu.make_async_copy(
            (wg, wu)[m].at[0, pl.ds(start, WIDE[d]), :],
            wbuf.at[pl.ds(u % 3 * W0, WIDE[d]), :], wsem.at[u % 3],
        )

    def grad_copies(j, slot):
        start = pl.multiple_of(j * KB, KB)
        return [
            pltpu.make_async_copy(
                w.at[0, pl.ds(start, KB), :],
                wbuf.at[pl.ds(pl.multiple_of((slot * 2 + m) * KB, KB), KB), :], gsem.at[slot, m],
            )
            for m, w in enumerate((wg, wu))
        ]

    for u in range(3):
        fwd_copy(u).start()
    wd_copy().start()

    def group_rows(grp, c, n):
        return pl.ds(pl.multiple_of(grp * R + c * n, 16), n)

    def block(a, e):
        return part.at[T - 1, pl.ds(pl.multiple_of(a * R + e * C, 16), C), :]

    def a2a_copy(a, k):
        return pltpu.make_async_remote_copy(
            src_ref=block(a, (s + k) % E),
            dst_ref=X.at[a, tp, group_rows(g, k, C), :],
            send_sem=a2a_s.at[a, k], recv_sem=a2a_r.at[a, k],
            device_id=tokdev(k), device_id_type=MESH,
        )

    def own_copy(a):
        return pltpu.make_async_copy(
            block(a, s), X.at[a, tp, group_rows(g, 0, C), :], a2a_r.at[a, 0]
        )

    def ring_copy(a, h, d, c, received=False):
        view = X.at[a, slice_at(h + 1 if received else h, d), group_rows(g, c, CR), part_lanes(d)]
        return pltpu.make_async_remote_copy(
            src_ref=view, dst_ref=view,
            send_sem=ring_s.at[a, h, d, c], recv_sem=ring_r.at[a, h, d, c],
            device_id=ringdev(d), device_id_type=MESH,
        )

    def pair_copy(a, h, d, c, received=False):
        view = X.at[a, slice_at(h, d), group_rows(other if received else g, c, CR), part_lanes(d)]
        return pltpu.make_async_remote_copy(
            src_ref=view, dst_ref=view,
            send_sem=pair_s.at[a, h, d, c], recv_sem=pair_r.at[a, h, d, c],
            device_id=pairdev, device_id_type=MESH,
        )

    def sq_copy(k):
        return pltpu.make_async_remote_copy(
            src_ref=sq.at[0], dst_ref=sq.at[k], send_sem=sq_s.at[k], recv_sem=sq_r.at[k],
            device_id={"tp": (tp + k) % T}, device_id_type=MESH,
        )

    def doc_copy(k):
        return pltpu.make_async_remote_copy(
            src_ref=doc.at[0], dst_ref=doc.at[k], send_sem=doc_s.at[k], recv_sem=doc_r.at[k],
            device_id={"tok": (s + k // G) % E, "grp": (g + k % G) % G}, device_id_type=MESH,
        )

    def send_blocks(a):
        own_copy(a).start()
        for k in range(1, E):
            a2a_copy(a, k).start()

    def lane_sum(value):
        return jnp.sum(value, axis=1, keepdims=True)

    def exchange_sums():
        total = jnp.zeros((N, 128), F32)
        for n in range(W // 128):
            value = hidden[:, n * 128:(n + 1) * 128].astype(F32)
            total += value * value
        sq[0] = jnp.broadcast_to(lane_sum(total), (N, 128))
        counts = jnp.sum(docs[...].astype(F32), axis=0, keepdims=True)
        doc[0] = jnp.broadcast_to(counts, (8, 128))
        pl.semaphore_wait(barrier, 2 * (E - 1) + T)
        for k in range(1, T):
            sq_copy(k).start()
        for k in range(1, E * G):
            doc_copy(k).start()

    def place_rows():
        total = sq[0]
        for k in range(1, T):
            sq_copy(k).wait_recv()
            total += sq[k]
        scaling = lax.rsqrt(total / D + 1e-05)
        where = placing[...]
        for n in range(W // 128):
            cols = slice(n * 128, (n + 1) * 128)
            normed = (hidden[:, cols].astype(F32) * scaling * gain[:, cols].astype(F32)).astype(BF16)
            part[T - 1, 0:R, cols] = jnp.dot(where, normed, preferred_element_type=F32).astype(BF16)

    def place_cot():
        lengths = doc[0]
        for k in range(1, E * G):
            doc_copy(k).wait_recv()
            lengths += doc[k]
        where = placing[...]
        slot_docs = jnp.dot(where, docs[...], preferred_element_type=F32)
        slot_len = lane_sum(slot_docs * lengths[0:1, :])
        weight = jnp.where(slot_len > 0.0, N / jnp.maximum(slot_len, 1.0), 0.0)
        scale = lane_sum(placed_gates[...]) * weight
        CW = tile_of(W, 256)
        for n in range(W // CW):
            cols = slice(n * CW, (n + 1) * CW)
            value = jnp.dot(where, upstream[:, cols], preferred_element_type=F32)
            part[T - 1, R:2 * R, cols] = (value * scale).astype(BF16)

    def combine():
        back_own().wait()
        for k in range(1, E):
            back_copy(k).wait_recv()
        CW = tile_of(W, 256)
        ways = []
        for k in range(picks.shape[0]):
            pick = picks[k]
            ways.append((jnp.where(pick != 0.0, 1.0, 0.0).astype(BF16), lane_sum(pick)))
        for n in range(W // CW):
            cols = slice(n * CW, (n + 1) * CW)
            total = jnp.zeros((N, CW), F32)
            for where, gate in ways:
                total += gate * jnp.dot(where, back[:, cols], preferred_element_type=F32)
            mixed[:, cols] = (hidden[:, cols].astype(F32) + total).astype(BF16)

    def arrive(a, h):
        for c in range(NC):
            for d in range(2):
                if h == 0:
                    per = E // NC
                    for k in range(c * per, (c + 1) * per) if d == 0 else ():
                        if k == 0:
                            own_copy(a).wait()
                        else:
                            a2a_copy(a, k).wait_recv()
                else:
                    ring_copy(a, h - 1, d, c, True).wait_recv()
                if h < T - 1:
                    ring_copy(a, h, d, c).start()
                pair_copy(a, h, d, c).start()

    def pair_arrive(a, h):
        for c in range(NC):
            for d in range(2):
                pair_copy(a, h, d, c, True).wait_recv()

    def lanes(start, n, unit=128):
        return pl.ds(pl.multiple_of(start, unit), n)

    HN = tile_of(H, 256)

    def zero(ref):
        def body(i, _):
            ref[pl.ds(pl.multiple_of(i * 16, 16), 16), :] = jnp.zeros((16, ref.shape[1]), F32)
            return 0
        lax.fori_loop(0, ref.shape[0] // 16, body, 0)

    def forward(h):
        pair_arrive(0, h)

        for u in range(4 * h, 4 * h + 4):
            d, acc = u // 2 % 2, (accg, accu)[u % 2]
            fwd_copy(u).wait()
            t = slice_at(h, d)

            def body(n, _, u=u, d=d, acc=acc, t=t):
                cols = lanes(n * HN, HN)
                acc[:, cols] += jnp.dot(
                    X[0, t, :, part_lanes(d)], wbuf[pl.ds(u % 3 * W0, WIDE[d]), cols],
                    preferred_element_type=F32,
                )
                return 0

            lax.fori_loop(0, H // HN, body, 0)
            if u + 3 < 4 * T:
                fwd_copy(u + 3).start()

    def activate():
        def body(i, _):
            rows = pl.ds(pl.multiple_of(i * 16, 16), 16)
            gate = accg[rows, :]
            up = accu[rows, :]
            sig = jax.nn.sigmoid(gate)
            silu = gate * sig
            act[rows, :] = (silu * up).astype(BF16)
            accg[rows, :] = up * sig * (1.0 + gate * (1.0 - sig))
            accu[rows, :] = silu
            return 0

        lax.fori_loop(0, G * R // 16, body, 0)
        for n in range(H // 128):
            act_t[n * 128:(n + 1) * 128, :] = act[:, n * 128:(n + 1) * 128].T

    def gradients():
        def body(i, _):
            rows = pl.ds(pl.multiple_of(i * 16, 16), 16)
            grad = ga[rows, :]
            dgu[rows, 0:H] = (grad * accg[rows, :]).astype(BF16)
            dgu[rows, H:2 * H] = (grad * accu[rows, :]).astype(BF16)
            return 0

        lax.fori_loop(0, G * R // 16, body, 0)

    def part_copy(k, d):
        return pltpu.make_async_remote_copy(
            src_ref=part.at[k, pl.ds(pl.multiple_of(other * R, 16), R), part_lanes(d)],
            dst_ref=part_in.at[k, :, part_lanes(d)],
            send_sem=part_s.at[k, d], recv_sem=part_r.at[k, d],
            device_id=pairdev, device_id_type=MESH,
        )

    def own_part(k, d):
        return part.at[k, pl.ds(pl.multiple_of(g * R, 16), R), part_lanes(d)]

    def down(k):
        for d in range(2):
            t = snake((p + (1 + k if d else T - 1 - k)) % T, T)
            WN = tile_of(WIDE[d], 256)

            def body(n, _, d=d, t=t, WN=WN):
                part[k, :, lanes(LOW[d] + n * WN, WN)] = jnp.dot(
                    act[...], wdv[:, lanes(t * W + LOW[d] + n * WN, WN)],
                    preferred_element_type=F32,
                ).astype(BF16)
                return 0

            lax.fori_loop(0, WIDE[d] // WN, body, 0)
            part_copy(k, d).start()

    def grad_act(h):
        pair_arrive(1, h)
        for d in range(2):
            t = slice_at(h, d)

            def body(n, _, d=d, t=t):
                ga[:, lanes(n * HN, HN)] += lax.dot_general(
                    X[1, t, :, part_lanes(d)],
                    wdv[pl.ds(pl.multiple_of(n * HN, 16), HN), lanes(t * W + LOW[d], WIDE[d])],
                    (((1,), (1,)), ((), ())), preferred_element_type=F32,
                )
                return 0

            lax.fori_loop(0, H // HN, body, 0)

    FT = tile_of(H, 512)

    def score_down(h, d):
        t = slice_at(h, d)
        WN = tile_of(WIDE[d], 256)

        def body(i, _):
            f = i // (WIDE[d] // WN)
            n = i % (WIDE[d] // WN)
            fr = pl.ds(pl.multiple_of(f * FT, 16), FT)
            grad = jnp.dot(
                act_t[fr, :], X[1, t, :, lanes(LOW[d] + n * WN, WN)], preferred_element_type=F32
            )
            value = jnp.abs(grad * wdv[fr, lanes(t * W + LOW[d] + n * WN, WN)].astype(F32))
            total = imp_dn[fr, :]
            for q in range(WN // 128):
                total += value[:, q * 128:(q + 1) * 128]
            imp_dn[fr, :] = total
            return 0

        lax.fori_loop(0, (H // FT) * (WIDE[d] // WN), body, 0)

    NU = D // KB

    def score_gate_up(first, last):
        def body(j, _):
            slot = j % 2

            @pl.when(j + 1 < NU)
            def _():
                for c in grad_copies(j + 1, 1 - slot):
                    c.start()

            for c in grad_copies(j, slot):
                c.wait()
            for q in range(KB // 128):
                xt[q * 128:(q + 1) * 128, :] = X[0, j // NK, :, lanes((j % NK) * KB + q * 128, 128)].T
            for m in range(2):
                for n in range(H // HN):
                    grad = jnp.dot(
                        xt[...], dgu[:, m * H + n * HN:m * H + (n + 1) * HN],
                        preferred_element_type=F32,
                    )
                    value = jnp.abs(grad * wbuf[pl.ds(pl.multiple_of((slot * 2 + m) * KB, KB), KB), n * HN:(n + 1) * HN].astype(F32))
                    imp_gu[:, n * HN:(n + 1) * HN] += jnp.sum(value.reshape(KB // 8, 8, HN), axis=0)
            return 0

        lax.fori_loop(first, last, body, 0)

    def sum_copy(k, d):
        return pltpu.make_async_remote_copy(
            src_ref=own_part(k, d), dst_ref=sum_in.at[k, :, part_lanes(d)],
            send_sem=sum_s.at[k, d], recv_sem=sum_r.at[k, d],
            device_id=ringdev(d), device_id_type=MESH,
        )

    def back_rows(k):
        return part.at[T - 1, pl.ds(pl.multiple_of(g * R + k * C, 16), C), :]

    def back_copy(k):
        return pltpu.make_async_remote_copy(
            src_ref=back_rows(k), dst_ref=back.at[pl.ds(pl.multiple_of(s * C, 16), C), :],
            send_sem=back_s.at[k], recv_sem=back_r.at[k],
            device_id={"tok": (s + E - k) % E}, device_id_type=MESH,
        )

    def back_own():
        return pltpu.make_async_copy(
            back_rows(0), back.at[pl.ds(pl.multiple_of(s * C, 16), C), :], back_r.at[0]
        )

    def reduce_step(k):
        for d in range(2):
            part_copy(k, d).wait_recv()
            if k > 0:
                sum_copy(k - 1, d).wait_recv()

            def body(i, _, cols=part_lanes(d)):
                rows = pl.ds(pl.multiple_of(g * R + i * 16, 16), 16)
                here = pl.ds(pl.multiple_of(i * 16, 16), 16)
                total = part[k, rows, cols].astype(F32) + part_in[k, here, cols].astype(F32)
                if k > 0:
                    total += sum_in[k - 1, here, cols].astype(F32)
                part[k, rows, cols] = total.astype(BF16)
                return 0

            lax.fori_loop(0, R // 16, body, 0)
            if k < T - 1:
                sum_copy(k, d).start()
        if k == T - 1:
            back_own().start()
            for q in range(1, E):
                back_copy(q).start()

    exchange_sums()
    for ref in (accg, accu, ga):
        zero(ref)
    imp_gu[...] = jnp.zeros(imp_gu.shape, F32)
    imp_dn[...] = jnp.zeros(imp_dn.shape, F32)
    place_rows()
    send_blocks(0)
    place_cot()

    arrive(0, 0)
    send_blocks(1)
    for h in range(1, T):
        arrive(0, h)
        forward(h - 1)
        if h == min(2, T - 1):
            arrive(1, 0)
    forward(T - 1)
    for c in grad_copies(0, 0):
        c.start()
    activate()
    wd_copy().wait()
    for a in range(2):
        for k in range(1, E):
            a2a_copy(a, k).wait_send()
    for h in range(1, T):
        down(h - 1)
        if h > 1:
            reduce_step(h - 2)
        arrive(1, h)
        grad_act(h - 1)
        for d in range(2):
            score_down(h - 1, d)
    down(T - 1)
    grad_act(T - 1)
    gradients()
    first, second = NU // 4, NU // 4 + NU // 3
    score_gate_up(0, first)
    reduce_step(T - 2)
    score_gate_up(first, second)
    reduce_step(T - 1)
    score_gate_up(second, NU)
    for d in range(2):
        score_down(T - 1, d)
    for n in range(H // 128):
        cols = slice(n * 128, (n + 1) * 128)
        value = jnp.sum(imp_gu[:, cols], axis=0, keepdims=True)
        value += jnp.sum(imp_dn[cols, :].T, axis=0, keepdims=True)
        imp[:, cols] = value / (N * E * G)
    combine()

    for k in range(1, E):
        back_copy(k).wait_send()
    for k in range(1, T):
        sq_copy(k).wait_send()
    for k in range(1, E * G):
        doc_copy(k).wait_send()
    for k in range(T):
        for d in range(2):
            part_copy(k, d).wait_send()
            if k < T - 1:
                sum_copy(k, d).wait_send()
            for a in range(2):
                for c in range(NC):
                    pair_copy(a, k, d, c).wait_send()
                    if k < T - 1:
                        ring_copy(a, k, d, c).wait_send()


def expert_call(hidden, gain, upstream, placing, placed_gates, docs, picks, w_gate, w_up, w_down):
    N, W = hidden.shape
    E = lax.axis_size("tok")
    C = placing.shape[0] // E
    T = lax.axis_size("tp")
    G = lax.axis_size("grp")
    H = w_gate.shape[2]
    D = w_gate.shape[1]
    NC = E if T <= 4 else 1
    KB = tile_of(W, 512)
    rows = G * E * C
    W0 = -(-W // 256) * 128
    dma = pltpu.SemaphoreType.DMA
    hbm = pl.BlockSpec(memory_space=pl.ANY)
    vmem = pl.BlockSpec(memory_space=pltpu.VMEM)
    return pl.pallas_call(
        functools.partial(expert_kernel, E, T, G, C, W, H, NC, KB),
        out_shape=(
            jax.ShapeDtypeStruct((N, W), BF16),
            jax.ShapeDtypeStruct((1, H), F32),
        ),
        in_specs=[vmem] * 7 + [hbm] * 3,
        out_specs=(vmem, vmem),
        scratch_shapes=[
            pltpu.VMEM((2, T, rows, W), BF16),
            pltpu.VMEM((rows, H), F32),
            pltpu.VMEM((rows, H), F32),
            pltpu.VMEM((rows, H), F32),
            pltpu.VMEM((rows, H), BF16),
            pltpu.VMEM((H, rows), BF16),
            pltpu.VMEM((rows, 2 * H), BF16),
            pltpu.VMEM((H, D), BF16),
            pltpu.VMEM((T, rows, W), BF16),
            pltpu.VMEM((T, E * C, W), BF16),
            pltpu.VMEM((T - 1, E * C, W), BF16),
            pltpu.VMEM((max(3 * W0, 4 * KB), H), BF16),
            pltpu.VMEM((KB, rows), BF16),
            pltpu.VMEM((8, H), F32),
            pltpu.VMEM((H, 128), F32),
            pltpu.VMEM((E * C, W), BF16),
            pltpu.VMEM((T, N, 128), F32),
            pltpu.VMEM((E * G, 8, 128), F32),
            dma((2, E)), dma((2, E)),
            dma((2, T, 2, NC)), dma((2, T, 2, NC)),
            dma((2, T, 2, NC)), dma((2, T, 2, NC)),
            dma((T, 2)), dma((T, 2)),
            dma((T, 2)), dma((T, 2)),
            dma((E,)), dma((E,)),
            dma((3,)), dma((2, 2)), dma,
            dma((T,)), dma((T,)), dma((E * G,)), dma((E * G,)),
        ],
        compiler_params=pltpu.CompilerParams(
            collective_id=0, has_side_effects=True, vmem_limit_bytes=64 * 1024 * 1024 - 65536
        ),
        cost_estimate=pl.CostEstimate(
            flops=14 * rows * D * H, bytes_accessed=6 * D * H * 2, transcendentals=rows * H
        ),
        name="expert_layer",
    )(hidden, gain, upstream, placing, placed_gates, docs, picks, w_gate, w_up, w_down)


def on_device(hidden, gain, expert_ids, gate_weights, segment_ids, upstream, w_gate, w_up, w_down):
    rows_here = hidden.shape[0]
    top_count = expert_ids.shape[1]
    experts = lax.axis_size("tok")
    groups = lax.axis_size("grp")
    capacity = -(-(5 * rows_here // (2 * experts)) // 16) * 16
    width = w_gate.shape[1]
    places = jnp.arange(rows_here, dtype=jnp.int32)
    earlier = places[None, :] < places[:, None]
    all_slots = jnp.arange(experts * capacity, dtype=jnp.int32)
    docs = (segment_ids[:, None] == jnp.arange(128, dtype=jnp.int32)[None, :]).astype(BF16)
    placed_gates = jnp.zeros((experts * capacity, rows_here), F32)
    placing = jnp.zeros((experts * capacity, rows_here), jnp.bool_)
    picks = []
    for k in range(top_count):
        same = jnp.zeros((rows_here, rows_here), jnp.bool_)
        for other in range(top_count):
            same |= expert_ids[:, k][:, None] == expert_ids[:, other][None, :]
        slot = jnp.sum((same & earlier).astype(jnp.int32), axis=1)
        target = expert_ids[:, k] * capacity + slot
        match = all_slots[:, None] == target[None, :]
        placing |= match
        placed_gates += jnp.where(match, gate_weights[:, k][None, :], 0.0)
        picks.append(jnp.where(target[:, None] == all_slots[None, :], gate_weights[:, k][:, None], 0.0))
    return expert_call(
        hidden, gain[None, :], upstream, placing.astype(BF16), placed_gates, docs, jnp.stack(picks),
        w_gate, w_up, w_down,
    )


def solution(mesh):
    placed = (
        P(("tok", "grp"), "tp"),
        P("tp"),
        P(("tok", "grp"), None),
        P(("tok", "grp"), None),
        P(("tok", "grp")),
        P(("tok", "grp"), "tp"),
        P("tok", None, ("tp", "grp")),
        P("tok", None, ("tp", "grp")),
        P("tok", ("tp", "grp"), None),
    )
    return jax.shard_map(
        on_device,
        mesh=mesh,
        in_specs=placed,
        out_specs=(P(("tok", "grp"), "tp"), P("tok", ("tp", "grp"))),
        check_vma=False,
    )
```

```python
import functools
import math

import jax
import jax.numpy as jnp
from jax import lax
from jax.experimental import pallas as pl
from jax.experimental.pallas import tpu as pltpu
from jax.sharding import PartitionSpec as P

MESH = pl.DeviceIdType.MESH
F32 = jnp.float32
BF16 = jnp.bfloat16


def snake(i, n):
    side = math.isqrt(n)
    if side * side != n:
        return i
    r = i // side
    q = i % side
    return r * side + q + (r % 2) * (side - 1 - 2 * q)


def tile_of(n, most):
    return most if n % most == 0 else n


def expert_kernel(
    E, T, G, C, W, H, NC, KB,
    hidden, gain, upstream, placing, placed_gates, docs, picks, wg, wu, wd,
    mixed, imp,
    X, accg, accu, ga, act, act_t, dgu, wdv, part, part_in, sum_in, wbuf, xt,
    imp_gu, imp_dn, back, sq, doc,
    a2a_s, a2a_r, ring_s, ring_r, pair_s, pair_r, part_s, part_r, sum_s, sum_r, back_s, back_r, wsem, gsem, wdsem,
    sq_s, sq_r, doc_s, doc_r,
):
    s = lax.axis_index("tok")
    tp = lax.axis_index("tp")
    g = lax.axis_index("grp")
    p = snake(tp, T)
    right = snake((p + 1) % T, T)
    left = snake((p + T - 1) % T, T)
    other = 1 - g
    R = E * C
    CR = R // NC
    D = T * W
    NK = W // KB
    N = hidden.shape[0]
    W0 = -(-W // 256) * 128
    LOW = (0, W0)
    WIDE = (W0, W - W0)

    def part_lanes(d):
        return slice(LOW[d], LOW[d] + WIDE[d])

    def tokdev(k):
        return {"tok": (s + k) % E}

    def ringdev(d):
        return {"tp": right if d == 0 else left}

    pairdev = {"grp": other}

    barrier = pltpu.get_barrier_semaphore()
    for k in range(1, E):
        pl.semaphore_signal(barrier, inc=1, device_id=tokdev(k), device_id_type=MESH)
        pl.semaphore_signal(
            barrier, inc=1, device_id={"tok": (s + k) % E, "grp": other}, device_id_type=MESH
        )
    for k in range(1, T):
        pl.semaphore_signal(barrier, inc=1, device_id={"tp": (tp + k) % T}, device_id_type=MESH)
    pl.semaphore_signal(barrier, inc=1, device_id=pairdev, device_id_type=MESH)

    def slice_at(h, d):
        return snake((p + (h if d else T - h)) % T, T)

    def wd_copy():
        return pltpu.make_async_copy(wd.at[0], wdv, wdsem)

    def fwd_copy(u):
        h, d, m = u // 4, u // 2 % 2, u % 2
        start = pl.multiple_of(slice_at(h, d) * W + LOW[d], 128)
        return pltpu.make_async_copy(
            (wg, wu)[m].at[0, pl.ds(start, WIDE[d]), :],
            wbuf.at[pl.ds(u % 3 * W0, WIDE[d]), :], wsem.at[u % 3],
        )

    def grad_copies(j, slot):
        start = pl.multiple_of(j * KB, KB)
        return [
            pltpu.make_async_copy(
                w.at[0, pl.ds(start, KB), :],
                wbuf.at[pl.ds(pl.multiple_of((slot * 2 + m) * KB, KB), KB), :], gsem.at[slot, m],
            )
            for m, w in enumerate((wg, wu))
        ]

    for u in range(3):
        fwd_copy(u).start()
    wd_copy().start()

    def group_rows(grp, c, n):
        return pl.ds(pl.multiple_of(grp * R + c * n, 16), n)

    def block(a, e):
        return part.at[T - 1, pl.ds(pl.multiple_of(a * R + e * C, 16), C), :]

    def a2a_copy(a, k):
        return pltpu.make_async_remote_copy(
            src_ref=block(a, (s + k) % E),
            dst_ref=X.at[a, tp, group_rows(g, k, C), :],
            send_sem=a2a_s.at[a, k], recv_sem=a2a_r.at[a, k],
            device_id=tokdev(k), device_id_type=MESH,
        )

    def own_copy(a):
        return pltpu.make_async_copy(
            block(a, s), X.at[a, tp, group_rows(g, 0, C), :], a2a_r.at[a, 0]
        )

    def ring_copy(a, h, d, c, received=False):
        view = X.at[a, slice_at(h + 1 if received else h, d), group_rows(g, c, CR), part_lanes(d)]
        return pltpu.make_async_remote_copy(
            src_ref=view, dst_ref=view,
            send_sem=ring_s.at[a, h, d, c], recv_sem=ring_r.at[a, h, d, c],
            device_id=ringdev(d), device_id_type=MESH,
        )

    def pair_copy(a, h, d, c, received=False):
        view = X.at[a, slice_at(h, d), group_rows(other if received else g, c, CR), part_lanes(d)]
        return pltpu.make_async_remote_copy(
            src_ref=view, dst_ref=view,
            send_sem=pair_s.at[a, h, d, c], recv_sem=pair_r.at[a, h, d, c],
            device_id=pairdev, device_id_type=MESH,
        )

    def sq_copy(k):
        return pltpu.make_async_remote_copy(
            src_ref=sq.at[0], dst_ref=sq.at[k], send_sem=sq_s.at[k], recv_sem=sq_r.at[k],
            device_id={"tp": (tp + k) % T}, device_id_type=MESH,
        )

    def doc_copy(k):
        return pltpu.make_async_remote_copy(
            src_ref=doc.at[0], dst_ref=doc.at[k], send_sem=doc_s.at[k], recv_sem=doc_r.at[k],
            device_id={"tok": (s + k // G) % E, "grp": (g + k % G) % G}, device_id_type=MESH,
        )

    def send_blocks(a):
        for k in range(1, E):
            a2a_copy(a, k).start()

    def lane_sum(value):
        return jnp.sum(value, axis=1, keepdims=True)

    def exchange_sums():
        total = jnp.zeros((N, 128), F32)
        for n in range(W // 128):
            value = hidden[:, n * 128:(n + 1) * 128].astype(F32)
            total += value * value
        sq[0] = jnp.broadcast_to(lane_sum(total), (N, 128))
        counts = jnp.sum(docs[...].astype(F32), axis=0, keepdims=True)
        doc[0] = jnp.broadcast_to(counts, (8, 128))
        pl.semaphore_wait(barrier, 2 * (E - 1) + T)
        for k in range(1, T):
            sq_copy(k).start()
        for k in range(1, E * G):
            doc_copy(k).start()

    def place_rows():
        total = sq[0]
        for k in range(1, T):
            sq_copy(k).wait_recv()
            total += sq[k]
        scaling = lax.rsqrt(total / D + 1e-05)
        where = placing[...]
        for n in range(W // 128):
            cols = slice(n * 128, (n + 1) * 128)
            normed = (hidden[:, cols].astype(F32) * scaling * gain[:, cols].astype(F32)).astype(BF16)
            part[T - 1, 0:R, cols] = jnp.dot(where, normed, preferred_element_type=F32).astype(BF16)

    def place_cot():
        lengths = doc[0]
        for k in range(1, E * G):
            doc_copy(k).wait_recv()
            lengths += doc[k]
        where = placing[...]
        slot_docs = jnp.dot(where, docs[...], preferred_element_type=F32)
        slot_len = lane_sum(slot_docs * lengths[0:1, :])
        weight = jnp.where(slot_len > 0.0, N / jnp.maximum(slot_len, 1.0), 0.0)
        scale = lane_sum(placed_gates[...]) * weight
        CW = tile_of(W, 256)
        for n in range(W // CW):
            cols = slice(n * CW, (n + 1) * CW)
            value = jnp.dot(where, upstream[:, cols], preferred_element_type=F32)
            part[T - 1, R:2 * R, cols] = (value * scale).astype(BF16)

    def combine():
        back_own().wait()
        for k in range(1, E):
            back_copy(k).wait_recv()
        CW = tile_of(W, 256)
        ways = []
        for k in range(picks.shape[0]):
            pick = picks[k]
            ways.append((jnp.where(pick != 0.0, 1.0, 0.0).astype(BF16), lane_sum(pick)))
        for n in range(W // CW):
            cols = slice(n * CW, (n + 1) * CW)
            total = jnp.zeros((N, CW), F32)
            for where, gate in ways:
                total += gate * jnp.dot(where, back[:, cols], preferred_element_type=F32)
            mixed[:, cols] = (hidden[:, cols].astype(F32) + total).astype(BF16)

    def arrive(a, h, c):
        if h == 0:
            for k in range(c * (E // NC), (c + 1) * (E // NC)):
                if k == 0:
                    own_copy(a).wait()
                else:
                    a2a_copy(a, k).wait_recv()
        for d in range(2):
            if h > 0:
                ring_copy(a, h - 1, d, c, True).wait_recv()
            if h < T - 1:
                ring_copy(a, h, d, c).start()
            pair_copy(a, h, d, c).start()

    def pair_arrive(a, h):
        for c in range(NC):
            for d in range(2):
                pair_copy(a, h, d, c, True).wait_recv()

    def lanes(start, n, unit=128):
        return pl.ds(pl.multiple_of(start, unit), n)

    HN = tile_of(H, 256)

    def zero(ref):
        def body(i, _):
            ref[pl.ds(pl.multiple_of(i * 16, 16), 16), :] = jnp.zeros((16, ref.shape[1]), F32)
            return 0
        lax.fori_loop(0, ref.shape[0] // 16, body, 0)

    def forward(h):
        pair_arrive(0, h)

        for u in range(4 * h, 4 * h + 4):
            d, acc = u // 2 % 2, (accg, accu)[u % 2]
            fwd_copy(u).wait()
            t = slice_at(h, d)

            def body(n, _, u=u, d=d, acc=acc, t=t):
                cols = lanes(n * HN, HN)
                acc[:, cols] += jnp.dot(
                    X[0, t, :, part_lanes(d)], wbuf[pl.ds(u % 3 * W0, WIDE[d]), cols],
                    preferred_element_type=F32,
                )
                return 0

            lax.fori_loop(0, H // HN, body, 0)
            if u + 3 < 4 * T:
                fwd_copy(u + 3).start()

    def activate():
        def body(i, _):
            rows = pl.ds(pl.multiple_of(i * 16, 16), 16)
            gate = accg[rows, :]
            up = accu[rows, :]
            sig = jax.nn.sigmoid(gate)
            silu = gate * sig
            act[rows, :] = (silu * up).astype(BF16)
            accg[rows, :] = up * sig * (1.0 + gate * (1.0 - sig))
            accu[rows, :] = silu
            return 0

        lax.fori_loop(0, G * R // 16, body, 0)
        for n in range(H // 128):
            act_t[n * 128:(n + 1) * 128, :] = act[:, n * 128:(n + 1) * 128].T

    def gradients():
        def body(i, _):
            rows = pl.ds(pl.multiple_of(i * 16, 16), 16)
            grad = ga[rows, :]
            dgu[rows, 0:H] = (grad * accg[rows, :]).astype(BF16)
            dgu[rows, H:2 * H] = (grad * accu[rows, :]).astype(BF16)
            return 0

        lax.fori_loop(0, G * R // 16, body, 0)

    def part_copy(k, d):
        return pltpu.make_async_remote_copy(
            src_ref=part.at[k, pl.ds(pl.multiple_of(other * R, 16), R), part_lanes(d)],
            dst_ref=part_in.at[k, :, part_lanes(d)],
            send_sem=part_s.at[k, d], recv_sem=part_r.at[k, d],
            device_id=pairdev, device_id_type=MESH,
        )

    def own_part(k, d):
        return part.at[k, pl.ds(pl.multiple_of(g * R, 16), R), part_lanes(d)]

    def down(k):
        for d in range(2):
            t = snake((p + (1 + k if d else T - 1 - k)) % T, T)
            WN = tile_of(WIDE[d], 256)

            def body(n, _, d=d, t=t, WN=WN):
                part[k, :, lanes(LOW[d] + n * WN, WN)] = jnp.dot(
                    act[...], wdv[:, lanes(t * W + LOW[d] + n * WN, WN)],
                    preferred_element_type=F32,
                ).astype(BF16)
                return 0

            lax.fori_loop(0, WIDE[d] // WN, body, 0)
            part_copy(k, d).start()

    def grad_act(h):
        pair_arrive(1, h)
        for d in range(2):
            t = slice_at(h, d)

            def body(n, _, d=d, t=t):
                ga[:, lanes(n * HN, HN)] += lax.dot_general(
                    X[1, t, :, part_lanes(d)],
                    wdv[pl.ds(pl.multiple_of(n * HN, 16), HN), lanes(t * W + LOW[d], WIDE[d])],
                    (((1,), (1,)), ((), ())), preferred_element_type=F32,
                )
                return 0

            lax.fori_loop(0, H // HN, body, 0)

    FT = tile_of(H, 512)

    def score_down(h, d):
        t = slice_at(h, d)
        WN = tile_of(WIDE[d], 256)

        def body(i, _):
            f = i // (WIDE[d] // WN)
            n = i % (WIDE[d] // WN)
            fr = pl.ds(pl.multiple_of(f * FT, 16), FT)
            grad = jnp.dot(
                act_t[fr, :], X[1, t, :, lanes(LOW[d] + n * WN, WN)], preferred_element_type=F32
            )
            value = jnp.abs(grad * wdv[fr, lanes(t * W + LOW[d] + n * WN, WN)].astype(F32))
            total = imp_dn[fr, :]
            for q in range(WN // 128):
                total += value[:, q * 128:(q + 1) * 128]
            imp_dn[fr, :] = total
            return 0

        lax.fori_loop(0, (H // FT) * (WIDE[d] // WN), body, 0)

    NU = D // KB

    def score_gate_up(first, last):
        def body(j, _):
            slot = j % 2

            @pl.when(j + 1 < NU)
            def _():
                for c in grad_copies(j + 1, 1 - slot):
                    c.start()

            for c in grad_copies(j, slot):
                c.wait()
            for q in range(KB // 128):
                xt[q * 128:(q + 1) * 128, :] = X[0, j // NK, :, lanes((j % NK) * KB + q * 128, 128)].T
            for m in range(2):
                for n in range(H // HN):
                    grad = jnp.dot(
                        xt[...], dgu[:, m * H + n * HN:m * H + (n + 1) * HN],
                        preferred_element_type=F32,
                    )
                    value = jnp.abs(grad * wbuf[pl.ds(pl.multiple_of((slot * 2 + m) * KB, KB), KB), n * HN:(n + 1) * HN].astype(F32))
                    imp_gu[:, n * HN:(n + 1) * HN] += jnp.sum(value.reshape(KB // 8, 8, HN), axis=0)
            return 0

        lax.fori_loop(first, last, body, 0)

    def sum_copy(k, d):
        return pltpu.make_async_remote_copy(
            src_ref=own_part(k, d), dst_ref=sum_in.at[k, :, part_lanes(d)],
            send_sem=sum_s.at[k, d], recv_sem=sum_r.at[k, d],
            device_id=ringdev(d), device_id_type=MESH,
        )

    def back_rows(k):
        return part.at[T - 1, pl.ds(pl.multiple_of(g * R + k * C, 16), C), :]

    def back_copy(k):
        return pltpu.make_async_remote_copy(
            src_ref=back_rows(k), dst_ref=back.at[pl.ds(pl.multiple_of(s * C, 16), C), :],
            send_sem=back_s.at[k], recv_sem=back_r.at[k],
            device_id={"tok": (s + E - k) % E}, device_id_type=MESH,
        )

    def back_own():
        return pltpu.make_async_copy(
            back_rows(0), back.at[pl.ds(pl.multiple_of(s * C, 16), C), :], back_r.at[0]
        )

    def reduce_step(k):
        for d in range(2):
            part_copy(k, d).wait_recv()
            if k > 0:
                sum_copy(k - 1, d).wait_recv()

            def body(i, _, cols=part_lanes(d)):
                rows = pl.ds(pl.multiple_of(g * R + i * 16, 16), 16)
                here = pl.ds(pl.multiple_of(i * 16, 16), 16)
                total = part[k, rows, cols].astype(F32) + part_in[k, here, cols].astype(F32)
                if k > 0:
                    total += sum_in[k - 1, here, cols].astype(F32)
                part[k, rows, cols] = total.astype(BF16)
                return 0

            lax.fori_loop(0, R // 16, body, 0)
            if k < T - 1:
                sum_copy(k, d).start()
        if k == T - 1:
            back_own().start()
            for q in range(1, E):
                back_copy(q).start()

    exchange_sums()
    for ref in (accg, accu, ga):
        zero(ref)
    imp_gu[...] = jnp.zeros(imp_gu.shape, F32)
    imp_dn[...] = jnp.zeros(imp_dn.shape, F32)
    place_rows()
    own_copy(0).start()
    send_blocks(0)
    place_cot()
    own_copy(1).start()

    rows_first = [(3 * c + h, 0, h, c) for c in range(NC) for h in range(T)]
    rows_first += [(h + 1.5, 1, h, 0) for h in range(T)]
    for _, a, h, c in sorted(rows_first):
        if (a, h, c) == (0, T - 1, NC - 1):
            forward(0)
        arrive(a, h, c)
        if (a, h, c) == (0, 0, NC - 1):
            send_blocks(1)
    later = [(h, c) for _, h, c in sorted((3 * c + h, h, c) for c in range(1, NC) for h in range(T))]

    def arrive_next(n):
        for h, c in later[:n]:
            arrive(1, h, c)
        del later[:n]

    arrive_next(1)
    for h in range(1, T):
        forward(h)
        arrive_next(2)
    for c in grad_copies(0, 0):
        c.start()
    activate()
    arrive_next(2)
    wd_copy().wait()
    for k in range(T - 1):
        down(k)
        arrive_next(1)
        if k == 1:
            reduce_step(0)
    arrive_next(len(later))
    for a in range(2):
        for k in range(1, E):
            a2a_copy(a, k).wait_send()
    down(T - 1)
    for h in range(T):
        grad_act(h)
        if 0 < h < T - 2:
            reduce_step(h)
    gradients()
    first, second = NU // 4, NU // 4 + NU // 3
    score_gate_up(0, first)
    reduce_step(T - 2)
    score_gate_up(first, second)
    reduce_step(T - 1)
    score_gate_up(second, NU)
    for h in range(T):
        for d in range(2):
            score_down(h, d)
    for n in range(H // 128):
        cols = slice(n * 128, (n + 1) * 128)
        value = jnp.sum(imp_gu[:, cols], axis=0, keepdims=True)
        value += jnp.sum(imp_dn[cols, :].T, axis=0, keepdims=True)
        imp[:, cols] = value / (N * E * G)
    combine()

    for k in range(1, E):
        back_copy(k).wait_send()
    for k in range(1, T):
        sq_copy(k).wait_send()
    for k in range(1, E * G):
        doc_copy(k).wait_send()
    for k in range(T):
        for d in range(2):
            part_copy(k, d).wait_send()
            if k < T - 1:
                sum_copy(k, d).wait_send()
            for a in range(2):
                for c in range(NC):
                    pair_copy(a, k, d, c).wait_send()
                    if k < T - 1:
                        ring_copy(a, k, d, c).wait_send()


def expert_call(hidden, gain, upstream, placing, placed_gates, docs, picks, w_gate, w_up, w_down):
    N, W = hidden.shape
    E = lax.axis_size("tok")
    C = placing.shape[0] // E
    T = lax.axis_size("tp")
    G = lax.axis_size("grp")
    H = w_gate.shape[2]
    D = w_gate.shape[1]
    NC = E if T <= 4 else 1
    KB = tile_of(W, 512)
    rows = G * E * C
    W0 = -(-W // 256) * 128
    dma = pltpu.SemaphoreType.DMA
    hbm = pl.BlockSpec(memory_space=pl.ANY)
    vmem = pl.BlockSpec(memory_space=pltpu.VMEM)
    return pl.pallas_call(
        functools.partial(expert_kernel, E, T, G, C, W, H, NC, KB),
        out_shape=(
            jax.ShapeDtypeStruct((N, W), BF16),
            jax.ShapeDtypeStruct((1, H), F32),
        ),
        in_specs=[vmem] * 7 + [hbm] * 3,
        out_specs=(vmem, vmem),
        scratch_shapes=[
            pltpu.VMEM((2, T, rows, W), BF16),
            pltpu.VMEM((rows, H), F32),
            pltpu.VMEM((rows, H), F32),
            pltpu.VMEM((rows, H), F32),
            pltpu.VMEM((rows, H), BF16),
            pltpu.VMEM((H, rows), BF16),
            pltpu.VMEM((rows, 2 * H), BF16),
            pltpu.VMEM((H, D), BF16),
            pltpu.VMEM((T, rows, W), BF16),
            pltpu.VMEM((T, E * C, W), BF16),
            pltpu.VMEM((T - 1, E * C, W), BF16),
            pltpu.VMEM((max(3 * W0, 4 * KB), H), BF16),
            pltpu.VMEM((KB, rows), BF16),
            pltpu.VMEM((8, H), F32),
            pltpu.VMEM((H, 128), F32),
            pltpu.VMEM((E * C, W), BF16),
            pltpu.VMEM((T, N, 128), F32),
            pltpu.VMEM((E * G, 8, 128), F32),
            dma((2, E)), dma((2, E)),
            dma((2, T, 2, NC)), dma((2, T, 2, NC)),
            dma((2, T, 2, NC)), dma((2, T, 2, NC)),
            dma((T, 2)), dma((T, 2)),
            dma((T, 2)), dma((T, 2)),
            dma((E,)), dma((E,)),
            dma((3,)), dma((2, 2)), dma,
            dma((T,)), dma((T,)), dma((E * G,)), dma((E * G,)),
        ],
        compiler_params=pltpu.CompilerParams(
            collective_id=0, has_side_effects=True, vmem_limit_bytes=64 * 1024 * 1024 - 65536
        ),
        cost_estimate=pl.CostEstimate(
            flops=14 * rows * D * H, bytes_accessed=6 * D * H * 2, transcendentals=rows * H
        ),
        name="expert_layer",
    )(hidden, gain, upstream, placing, placed_gates, docs, picks, w_gate, w_up, w_down)


def on_device(hidden, gain, expert_ids, gate_weights, segment_ids, upstream, w_gate, w_up, w_down):
    rows_here = hidden.shape[0]
    top_count = expert_ids.shape[1]
    experts = lax.axis_size("tok")
    groups = lax.axis_size("grp")
    capacity = -(-(5 * rows_here // (2 * experts)) // 16) * 16
    width = w_gate.shape[1]
    places = jnp.arange(rows_here, dtype=jnp.int32)
    earlier = places[None, :] < places[:, None]
    all_slots = jnp.arange(experts * capacity, dtype=jnp.int32)
    docs = (segment_ids[:, None] == jnp.arange(128, dtype=jnp.int32)[None, :]).astype(BF16)
    placed_gates = jnp.zeros((experts * capacity, rows_here), F32)
    placing = jnp.zeros((experts * capacity, rows_here), jnp.bool_)
    picks = []
    for k in range(top_count):
        same = jnp.zeros((rows_here, rows_here), jnp.bool_)
        for other in range(top_count):
            same |= expert_ids[:, k][:, None] == expert_ids[:, other][None, :]
        slot = jnp.sum((same & earlier).astype(jnp.int32), axis=1)
        target = expert_ids[:, k] * capacity + slot
        match = all_slots[:, None] == target[None, :]
        placing |= match
        placed_gates += jnp.where(match, gate_weights[:, k][None, :], 0.0)
        picks.append(jnp.where(target[:, None] == all_slots[None, :], gate_weights[:, k][:, None], 0.0))
    return expert_call(
        hidden, gain[None, :], upstream, placing.astype(BF16), placed_gates, docs, jnp.stack(picks),
        w_gate, w_up, w_down,
    )


def solution(mesh):
    placed = (
        P(("tok", "grp"), "tp"),
        P("tp"),
        P(("tok", "grp"), None),
        P(("tok", "grp"), None),
        P(("tok", "grp")),
        P(("tok", "grp"), "tp"),
        P("tok", None, ("tp", "grp")),
        P("tok", None, ("tp", "grp")),
        P("tok", ("tp", "grp"), None),
    )
    return jax.shard_map(
        on_device,
        mesh=mesh,
        in_specs=placed,
        out_specs=(P(("tok", "grp"), "tp"), P("tok", ("tp", "grp"))),
        check_vma=False,
    )
```
